32 devices in a mesh: gx: 4 (over y, x), gy: 8 (over z, core).
Axes of the slice: x: 2, y: 2, z: 4, core: 2. Of those that a mesh axis runs over, the one named last changes fastest.
Arguments:
- positions: float32 [4, 8, 3, 256], P('gx', 'gy'), may hold values from 0 to 1
- species: int32 [4, 8, 256], P('gx', 'gy'), may hold values from 0 to 88
- dest_key: int32 [4, 8, 256], P('gx', 'gy'), may hold values from 0 to 4, as said below
- send_list: int32 [4, 8, 4, 32], P('gx', 'gy'), may hold values from 0 to 255, as said below
- send_count: int32 [4, 8, 4], P('gx', 'gy'), may hold values from 8 to 32, as said below
- border: int32 [4, 8, 128], P('gx', 'gy'), may hold values from 0 to 255, as said below
- neighbours: int32 [4, 8, 384, 12], P('gx', 'gy'), may hold values from -1 to 1535, as said below
- embedding: float32 [89, 128], replicated, may hold values from -4 to 4
- radial_in: float32 [2, 8, 64], replicated, may hold values from -2 to 2
- radial_mid: float32 [2, 64, 64], replicated, may hold values from -0.75 to 0.75
- radial_out_one: float32 [64, 384], replicated, may hold values from -4 to 4
- radial_out_two: float32 [64, 896], replicated, may hold values from -4 to 4
- mix: float32 [2, 3, 128, 128], replicated, may hold values from -0.5 to 0.5
- mix_out_one: float32 [3, 128, 128], replicated, may hold values from -0.5 to 0.5
- mix_out_two: float32 [128, 128], replicated, may hold values from -0.5 to 0.5
- product_one: float32 [5, 128], replicated, may hold values from -4 to 4
- product_two: float32 [3, 128], replicated, may hold values from -4 to 4
- read_lin: float32 [128], replicated, may hold values from -0.5 to 0.5
- read_hidden: float32 [128, 16], replicated, may hold values from -0.5 to 0.5
- read_out: float32 [16], replicated, may hold values from -1.5 to 1.5
Outputs:
- atom_energy: float32 [4, 8, 384], P('gx', 'gy')
- forces: float32 [4, 8, 3, 384], P('gx', 'gy')
The draws below stay inside these ranges and needn't reach their ends.
Inputs may be any that keep to these rules, and one draw needn't show every extreme that they name: `dest_key`: 0 keeps the atom; 1, 2, 3, 4 send it to the next device along gx, the previous along gx, the next along gy, the previous along gy (periodic); each device has at most 32 atoms of each nonzero key. `send_list`: row d holds in increasing order the slots whose dest_key is d + 1, then other slots as padding. `send_count`: the number of slots whose dest_key is d + 1; some device has exactly 32 in some direction in every draw. `border`: distinct slots whose dest_key is 0. `neighbours`: -1 marks an empty slot; a value below 384 is a local row after migration; 384 + (3 * a + b) * 128 + k is the k-th border row of the device at offset (a - 1, b - 1) along (gx, gy), with (a, b) never (1, 1); devices differ in how many slots are empty.
All inputs are finite; a program needn't handle non-finite values.
Results may differ from the reference program's by a relative error of at most 0.003.
Values may be sent and summed in bfloat16 or wider, within the bound.
A program may use at most 192 MiB of HBM per device.

```python
import math
import jax
import jax.numpy as jnp
from jax import lax

C = 128
H = 64
NB = 8
NELEM = 89
RH = 16
K = 12
M = 32
B = 128
A_OWN = 256
R = 384
GRID_X = 4
GRID_Y = 8
N_GX = 4
N_GY = 8


def migration_plan(key):
    device_total = GRID_X * GRID_Y
    count_key, hot_key, order_key = jax.random.split(key, 3)
    counts = jax.random.randint(count_key, (device_total * 4,), M // 4, M + 1)
    hottest = jax.random.randint(hot_key, (), 0, device_total * 4)
    counts = jnp.where(jnp.arange(device_total * 4) == hottest, M, counts).reshape(device_total, 4).astype(jnp.int32)
    orders = jax.vmap(lambda sub_key: jax.random.permutation(sub_key, A_OWN))(jax.random.split(order_key, device_total))
    limits = jnp.cumsum(counts, axis=1)
    places = jnp.arange(A_OWN)
    passed = jnp.sum((places[None, None, :] >= limits[:, :, None]).astype(jnp.int32), axis=1)
    label_at = jnp.where(places[None, :] < limits[:, 3:4], passed + 1, 0).astype(jnp.int32)
    labels = jax.vmap(lambda order, label: jnp.zeros((A_OWN,), jnp.int32).at[order].set(label))(orders, label_at)
    listed = jnp.stack([jnp.argsort((labels != target + 1).astype(jnp.int32), axis=1, stable=True)[:, :M] for target in range(4)], axis=1).astype(jnp.int32)
    border_rows = orders[:, A_OWN - B:].astype(jnp.int32)
    return (labels, listed, counts, border_rows)


def draw_dest_key(key, part):
    labels, listed, counts, border_rows = migration_plan(key)
    return labels.reshape(GRID_X, GRID_Y, A_OWN)


def draw_send_list(key, part):
    labels, listed, counts, border_rows = migration_plan(key)
    return listed.reshape(GRID_X, GRID_Y, 4, M)


def draw_send_count(key, part):
    labels, listed, counts, border_rows = migration_plan(key)
    return counts.reshape(GRID_X, GRID_Y, 4)


def draw_border(key, part):
    labels, listed, counts, border_rows = migration_plan(key)
    return border_rows.reshape(GRID_X, GRID_Y, B)


def draw_neighbours(key, part):
    key = jax.random.fold_in(key, 7)
    device_total = GRID_X * GRID_Y
    level_key, valid_key, ghost_key, block_key, inner_key, local_key = jax.random.split(key, 6)
    levels = jax.random.randint(level_key, (device_total, 1, 1), 2, 9)
    valid = jax.random.randint(valid_key, (device_total, R, K), 0, 8) < levels
    ghostly = jax.random.randint(ghost_key, (device_total, R, K), 0, 3) > 0
    blocks = jax.random.randint(block_key, (device_total, R, K), 0, 8)
    blocks = blocks + (blocks >= 4).astype(jnp.int32)
    ghost_index = R + blocks * B + jax.random.randint(inner_key, (device_total, R, K), 0, B)
    local_index = jax.random.randint(local_key, (device_total, R, K), 0, R)
    chosen = jnp.where(valid, jnp.where(ghostly, ghost_index, local_index), -1).astype(jnp.int32)
    chosen = chosen.at[0, 0, 0].set(R + 9 * B - 1)
    return chosen.reshape(GRID_X, GRID_Y, R, K)


def plant(result, key, low, largest):
    longest = result.shape.index(max(result.shape))
    spots = []
    for shift in (0, 1):
        where = [jax.random.randint(jax.random.fold_in(key, axis), (), 0, length) for axis, length in enumerate(result.shape)]
        where[longest] = (where[longest] + shift) % result.shape[longest]
        spots.append(tuple(where))
    return result.at[spots[0]].set(low).at[spots[1]].set(largest)


def level_of(key, shape, shards, smallest, high):
    factor_of = 1.0
    for dim, parts in shards:
        draws = jax.random.uniform(jax.random.fold_in(jax.random.fold_in(key, 6), dim), (parts,), jnp.float32, smallest / len(shards), high / len(shards))
        factor_of = factor_of * jnp.repeat(jnp.exp(draws), shape[dim] // parts).reshape((-1,) + (1,) * (len(shape) - 1 - dim))
    return factor_of


def gaussian(own_key, shape, deviation, reach, kind=jnp.bfloat16):
    return jnp.clip(deviation * jax.random.normal(own_key, shape, jnp.float32), -reach, reach).astype(kind)


def setup_inputs(seed: int = 0) -> dict:
    splits = jax.random.split(jax.random.key(seed), 21)
    return {
        "positions": jnp.clip(1.0 * jax.random.uniform(splits[0], (GRID_X, GRID_Y, 3, A_OWN), jnp.float32) ** level_of(splits[0], (GRID_X, GRID_Y, 3, A_OWN), ((0, 4), (1, 8)), -0.2, 0.2), 0.0, 1.0),
        "species": plant(jax.random.randint(splits[1], (GRID_X, GRID_Y, A_OWN), 0, NELEM), jax.random.fold_in(splits[1], 1), 0, NELEM - 1).astype(jnp.int32),
        "dest_key": draw_dest_key(jax.random.fold_in(splits[20], 71), 0),
        "send_list": draw_send_list(jax.random.fold_in(splits[20], 71), 0),
        "send_count": draw_send_count(jax.random.fold_in(splits[20], 71), 0),
        "border": draw_border(jax.random.fold_in(splits[20], 71), 0),
        "neighbours": draw_neighbours(jax.random.fold_in(splits[20], 71), 0),
        "embedding": gaussian(splits[7], (NELEM, C), 1.0, 4.0, jnp.float32),
        "radial_in": gaussian(splits[8], (2, NB, H), NB ** -0.5, 2.0, jnp.float32),
        "radial_mid": gaussian(splits[9], (2, H, H), H ** -0.5, 0.75, jnp.float32),
        "radial_out_one": gaussian(splits[10], (H, 3 * C), 1.0, 4.0, jnp.float32),
        "radial_out_two": gaussian(splits[11], (H, 7 * C), 1.0, 4.0, jnp.float32),
        "mix": gaussian(splits[12], (2, 3, C, C), C ** -0.5, 0.5, jnp.float32),
        "mix_out_one": gaussian(splits[13], (3, C, C), C ** -0.5, 0.5, jnp.float32),
        "mix_out_two": gaussian(splits[14], (C, C), C ** -0.5, 0.5, jnp.float32),
        "product_one": gaussian(splits[15], (5, C), 1.0, 4.0, jnp.float32),
        "product_two": gaussian(splits[16], (3, C), 1.0, 4.0, jnp.float32),
        "read_lin": gaussian(splits[17], (C,), C ** -0.5, 0.5, jnp.float32),
        "read_hidden": gaussian(splits[18], (C, RH), C ** -0.5, 0.5, jnp.float32),
        "read_out": gaussian(splits[19], (RH,), RH ** -0.5, 1.5, jnp.float32),
    }


cutoff_radius = 5.0
cell_side = 1.0
highest = lax.Precision.HIGHEST

def geometry(offsets, basis_count):
    squared = lax.optimization_barrier(jnp.sum(offsets * offsets, axis=0)) + 1.0
    distance = jnp.sqrt(squared)
    pointer = offsets / distance[None, :]
    scaled = distance / cutoff_radius
    sixth = scaled * scaled * scaled * scaled * scaled * scaled
    envelope = 1.0 - 28.0 * sixth + 48.0 * sixth * scaled - 21.0 * sixth * scaled * scaled
    orders = jnp.arange(1, basis_count + 1).astype(jnp.float32)[:, None]
    basis = math.sqrt(2.0 / cutoff_radius) * jnp.sin(orders * (math.pi / cutoff_radius) * distance[None, :]) * (envelope / distance)[None, :]
    along_x = pointer[0]
    along_y = pointer[1]
    along_z = pointer[2]
    root_five = math.sqrt(5.0)
    root_fifteen = math.sqrt(15.0)
    vector_part = math.sqrt(3.0) * pointer
    tensor_part = jnp.stack([root_fifteen * along_x * along_y, root_fifteen * along_y * along_z, 0.5 * root_five * (2.0 * along_z * along_z - along_x * along_x - along_y * along_y), root_fifteen * along_x * along_z, 0.5 * root_fifteen * (along_x * along_x - along_y * along_y)])
    return (basis, vector_part, tensor_part)

def radial(basis, w_in, w_mid, w_out):
    hidden = jax.nn.silu(jnp.dot(w_in.T, basis, precision=highest))
    hidden = jax.nn.silu(jnp.dot(w_mid.T, hidden, precision=highest))
    return jnp.dot(w_out.T, hidden, precision=highest)

def contract(matrix, values):
    return jnp.einsum('cd,...cn->...dn', matrix, values, precision=highest)

def interaction(first, pos_all, feats_all, occ_all, neighbour_block, pos_block, occ_block, residual, weights):
    w_in, w_mid, w_out, mixing, mixing_out, coefs = weights
    atoms, slots = neighbour_block.shape
    channels = mixing.shape[-1]
    flat_index = jnp.maximum(neighbour_block, 0).reshape(-1)
    edge_mask = (neighbour_block >= 0).astype(jnp.float32).reshape(-1) * occ_all[flat_index] * jnp.repeat(occ_block, slots)
    offsets = pos_all[:, flat_index] - jnp.repeat(pos_block, slots, axis=1)
    basis, vector_part, tensor_part = geometry(offsets, w_in.shape[0])
    source = feats_all[:, flat_index] * edge_mask[None, :]
    paths = 3 if first else 7
    edge_weights = radial(basis, w_in, w_mid, w_out).reshape(paths, channels, -1)
    scalar = source[:channels]
    if first:
        msg_scalar = edge_weights[0] * scalar
        msg_vector = edge_weights[1][None] * scalar[None] * vector_part[:, None]
        msg_tensor = edge_weights[2][None] * scalar[None] * tensor_part[:, None]
    else:
        vectors = source[channels:4 * channels].reshape(3, channels, -1)
        tensors = source[4 * channels:].reshape(5, channels, -1)
        msg_scalar = edge_weights[0] * scalar + edge_weights[1] * lax.optimization_barrier(jnp.sum(vector_part[:, None] * vectors, axis=0)) + edge_weights[2] * lax.optimization_barrier(jnp.sum(tensor_part[:, None] * tensors, axis=0))
        msg_vector = edge_weights[3][None] * scalar[None] * vector_part[:, None] + edge_weights[4][None] * vectors
        msg_tensor = edge_weights[5][None] * scalar[None] * tensor_part[:, None] + edge_weights[6][None] * tensors

    def pooling(message):
        return lax.optimization_barrier(jnp.sum(message.reshape(message.shape[:-1] + (atoms, slots)), axis=-1)) / slots
    mixed_scalar = contract(mixing[0], pooling(msg_scalar))
    mixed_vector = contract(mixing[1], pooling(msg_vector))
    mixed_tensor = contract(mixing[2], pooling(msg_tensor))
    product_scalar = mixed_scalar + coefs[0][:, None] * mixed_scalar * mixed_scalar + coefs[1][:, None] * lax.optimization_barrier(jnp.sum(mixed_vector * mixed_vector, axis=0)) + coefs[2][:, None] * lax.optimization_barrier(jnp.sum(mixed_tensor * mixed_tensor, axis=0))
    if first:
        product_vector = mixed_vector * (1.0 + coefs[3][:, None] * mixed_scalar)[None]
        product_tensor = mixed_tensor * (1.0 + coefs[4][:, None] * mixed_scalar)[None]
        new_scalar = contract(mixing_out[0], product_scalar) + residual
        new_vector = contract(mixing_out[1], product_vector).reshape(3 * channels, atoms)
        new_tensor = contract(mixing_out[2], product_tensor).reshape(5 * channels, atoms)
        return jnp.concatenate([new_scalar, new_vector, new_tensor], axis=0)
    return contract(mixing_out, product_scalar) + residual[:channels]

def run_layer(first, pos_all, feats_all, occ_all, occupied, neighbour_rows, weights):
    total_rows = neighbour_rows.shape[0]
    block_rows = math.gcd(total_rows, 128)
    block_count = total_rows // block_rows

    def one_block(block_index):
        start = block_index * block_rows
        neighbour_block = lax.dynamic_slice_in_dim(neighbour_rows, start, block_rows, 0)
        pos_block = lax.dynamic_slice_in_dim(pos_all, start, block_rows, 1)
        occ_block = lax.dynamic_slice_in_dim(occupied, start, block_rows, 0)
        residual = lax.dynamic_slice_in_dim(feats_all, start, block_rows, 1)
        return interaction(first, pos_all, feats_all, occ_all, neighbour_block, pos_block, occ_block, residual, weights)
    outputs = lax.map(jax.checkpoint(one_block), jnp.arange(block_count, dtype=jnp.int32))
    return jnp.moveaxis(outputs, 0, 1).reshape(outputs.shape[1], total_rows)

def shift_table():
    grid_shift = cell_side * (jnp.arange(3).astype(jnp.float32) - 1.0)
    first_axis = jnp.broadcast_to(grid_shift[:, None], (3, 3))
    second_axis = jnp.broadcast_to(grid_shift[None, :], (3, 3))
    return jnp.stack([first_axis, second_axis, jnp.zeros((3, 3), jnp.float32)], axis=-1)

def surround(table, grid_row, grid_column):
    blocks = []
    for across in range(3):
        line = []
        for alongside in range(3):
            line.append(table[(grid_row + across - 1) % N_GX, (grid_column + alongside - 1) % N_GY])
        blocks.append(jnp.stack(line))
    return jnp.stack(blocks)

def migrate(positions, species, dest_key, send_list, send_count):
    picked = jax.vmap(jax.vmap(lambda coords_row, listed: coords_row[:, listed]))(positions, send_list)
    picked_kinds = jax.vmap(jax.vmap(lambda kinds_row, listed: kinds_row[listed]))(species, send_list)
    slot_used = jnp.arange(send_list.shape[-1])[None, None, None, :] < send_count[..., None]
    picked_kinds = jnp.where(slot_used, picked_kinds, -1)
    arrival_moves = ((1, 0, 0), (-1, 0, 0), (1, 1, 1), (-1, 1, 1))
    coords_parts = [positions]
    kinds_parts = [species]
    occupied_parts = [(dest_key == 0).astype(jnp.float32)]
    for target in range(4):
        amount, grid_axis, coordinate = arrival_moves[target]
        moved = jnp.roll(picked[:, :, :, target], amount, axis=grid_axis)
        moved = moved.at[:, :, coordinate].add(-amount * cell_side)
        moved_kinds = jnp.roll(picked_kinds[:, :, target], amount, axis=grid_axis)
        coords_parts.append(moved)
        kinds_parts.append(moved_kinds)
        occupied_parts.append((moved_kinds >= 0).astype(jnp.float32))
    return (jnp.concatenate(coords_parts, axis=3), jnp.concatenate(kinds_parts, axis=2), jnp.concatenate(occupied_parts, axis=2))

def reference(positions, species, dest_key, send_list, send_count, border, neighbours, embedding, radial_in, radial_mid, radial_out_one, radial_out_two, mix, mix_out_one, mix_out_two, product_one, product_two, read_lin, read_hidden, read_out):
    coords, kinds, occupied = migrate(positions, species, dest_key, send_list, send_count)
    channels = embedding.shape[1]
    border_count = border.shape[-1]
    border_kinds = jax.vmap(jax.vmap(lambda kinds_row, rows_picked: kinds_row[rows_picked]))(kinds, border)
    first_weights = (radial_in[0], radial_mid[0], radial_out_one, mix[0], mix_out_one, product_one)
    second_weights = (radial_in[1], radial_mid[1], radial_out_two, mix[1], mix_out_two, product_two)
    offsets_grid = shift_table()
    device_total = N_GX * N_GY

    def total_energy(coords_in):
        border_coords = jax.vmap(jax.vmap(lambda coords_row, rows_picked: coords_row[:, rows_picked]))(coords_in, border)

        def assemble(device_index):
            grid_row = device_index // N_GY
            grid_column = device_index % N_GY
            beside_all = surround(border_coords, grid_row, grid_column) + offsets_grid[:, :, :, None]
            ghost = jnp.moveaxis(beside_all, 2, 0).reshape(3, 9 * border_count)
            pos_all = jnp.concatenate([coords_in[grid_row, grid_column], ghost], axis=1)
            occ_local = occupied[grid_row, grid_column]
            occ_all = jnp.concatenate([occ_local, jnp.ones((9 * border_count,), jnp.float32)])
            return (grid_row, grid_column, pos_all, occ_local, occ_all)

        def layer_one_device(device_index):
            grid_row, grid_column, pos_all, occ_local, occ_all = assemble(device_index)
            ghost_kinds = surround(border_kinds, grid_row, grid_column).reshape(9 * border_count)
            kinds_all = jnp.maximum(jnp.concatenate([kinds[grid_row, grid_column], ghost_kinds]), 0)
            initial = embedding[kinds_all].T
            return run_layer(True, pos_all, initial, occ_all, occ_local, neighbours[grid_row, grid_column], first_weights)
        hidden_all = lax.map(jax.checkpoint(layer_one_device), jnp.arange(device_total, dtype=jnp.int32))
        rounded = lax.optimization_barrier(hidden_all.astype(jnp.bfloat16)).astype(jnp.float32)
        hidden_used = hidden_all + lax.stop_gradient(rounded - hidden_all)
        hidden_grid = hidden_used.reshape((N_GX, N_GY) + hidden_used.shape[1:])
        border_feats = jax.vmap(jax.vmap(lambda feats_row, rows_picked: feats_row[:, rows_picked]))(hidden_grid, border)

        def layer_two_device(device_index):
            grid_row, grid_column, pos_all, occ_local, occ_all = assemble(device_index)
            beside_all = surround(border_feats, grid_row, grid_column)
            ghost = jnp.moveaxis(beside_all, 2, 0).reshape(beside_all.shape[2], 9 * border_count)
            table = jnp.concatenate([hidden_grid[grid_row, grid_column], ghost], axis=1)
            scalars = run_layer(False, pos_all, table, occ_all, occ_local, neighbours[grid_row, grid_column], second_weights)
            readout = jax.nn.silu(jnp.dot(read_hidden.T, scalars, precision=highest))
            return occ_local * jnp.dot(read_out, readout, precision=highest)
        energy_two = lax.map(jax.checkpoint(layer_two_device), jnp.arange(device_total, dtype=jnp.int32))
        energy_two = energy_two.reshape(N_GX, N_GY, -1)
        energy_one = occupied * jnp.einsum('c,xycr->xyr', read_lin, hidden_grid[:, :, :channels], precision=highest)
        atom_energy = energy_one + energy_two
        return (jnp.sum(atom_energy), atom_energy)
    (total_value, atom_energy), gradient = jax.value_and_grad(total_energy, has_aux=True)(coords)
    return (atom_energy, -gradient)
```

```python
import math

import jax
import jax.numpy as jnp
from jax import lax
from jax.experimental import pallas as pl
from jax.experimental.pallas import tpu as pltpu
from jax.sharding import PartitionSpec as P

f32 = jnp.float32
bf16 = jnp.bfloat16
highest = lax.Precision.HIGHEST
CUT = 5.0
L = 128
G = 256
CB = 16
VMEM_LIMIT = 56 * 1024 * 1024


def params():
    return pltpu.CompilerParams(vmem_limit_bytes=VMEM_LIMIT)


def dot(a, b):
    return jnp.dot(a, b, preferred_element_type=f32)


def dot_high(a, b):
    return jnp.dot(a, b, preferred_element_type=f32, precision=highest)


def hi_lo(x):
    hi = x.astype(bf16)
    return hi, (x - hi.astype(f32)).astype(bf16)


def dot_split(stack, x):
    hi, lo = hi_lo(x)
    return dot(stack, jnp.concatenate([hi, hi, lo], axis=0))


def silu(x):
    return x * jax.nn.sigmoid(x)


def silu_slope(x):
    sig = jax.nn.sigmoid(x)
    return sig * (1.0 + x * (1.0 - sig))


def geometry(ox, oy, oz):
    squared = ox * ox + oy * oy + oz * oz + 1.0
    distance = jnp.sqrt(squared)
    inverse = 1.0 / distance
    ux, uy, uz = ox * inverse, oy * inverse, oz * inverse
    t = distance / CUT
    sixth = t * t * t * t * t * t
    envelope = 1.0 - 28.0 * sixth + 48.0 * sixth * t - 21.0 * sixth * t * t
    orders = (lax.broadcasted_iota(jnp.int32, (8, ox.shape[1]), 0) + 1).astype(f32)
    wave = jnp.sin(orders * (math.pi / CUT) * jnp.broadcast_to(distance, orders.shape))
    scale = math.sqrt(2.0 / CUT) * envelope * inverse
    basis = wave * jnp.broadcast_to(scale, orders.shape)
    r3, r5, r15 = math.sqrt(3.0), math.sqrt(5.0), math.sqrt(15.0)
    harmonics = (
        r3 * ux,
        r3 * uy,
        r3 * uz,
        r15 * ux * uy,
        r15 * uy * uz,
        0.5 * r5 * (2.0 * uz * uz - ux * ux - uy * uy),
        r15 * ux * uz,
        0.5 * r15 * (ux * ux - uy * uy),
    )
    return basis, harmonics


def one_hot_columns(rows, index_row):
    place = lax.broadcasted_iota(jnp.int32, (rows, index_row.shape[1]), 0)
    return jnp.where(place == index_row, 1.0, 0.0).astype(bf16)


def one_hot_rows(index_column, base, columns):
    place = lax.broadcasted_iota(jnp.int32, (index_column.shape[0], columns), 1) + base
    return jnp.where(place == index_column, 1.0, 0.0).astype(bf16)


@jax.custom_vjp
def mixed(w, wt, x):
    return dot_split(wt, x)


def mixed_fwd(w, wt, x):
    return dot_split(wt, x), (w, wt)


def mixed_bwd(saved, g):
    w, wt = saved
    return None, None, dot_split(w, g)


mixed.defvjp(mixed_fwd, mixed_bwd)


def mix_orders(mats, mats_t, parts):
    scalar = mixed(mats[0], mats_t[0], parts[0])
    vector = mixed(mats[1], mats_t[1], jnp.concatenate(parts[1:4], axis=1))
    tensor = mixed(mats[2], mats_t[2], jnp.concatenate(parts[4:9], axis=1))
    return scalar, [vector[:, i * L : (i + 1) * L] for i in range(3)], [
        tensor[:, i * L : (i + 1) * L] for i in range(5)
    ]


def product_scalar(coefs, s, v, q):
    total = s + coefs[0] * s * s
    total = total + coefs[1] * (v[0] * v[0] + v[1] * v[1] + v[2] * v[2])
    return total + coefs[2] * (
        q[0] * q[0] + q[1] * q[1] + q[2] * q[2] + q[3] * q[3] + q[4] * q[4]
    )


def node_one(parts, mats, mats_t, outs, outs_t, coefs):
    s, v, q = mix_orders(mats, mats_t, parts)
    b0 = product_scalar(coefs, s, v, q)
    gate1 = 1.0 + coefs[3] * s
    gate2 = 1.0 + coefs[4] * s
    s, v, q = mix_orders(outs, outs_t, [b0] + [x * gate1 for x in v] + [x * gate2 for x in q])
    return [s] + v + q


def node_two(parts, residual, mats, mats_t, out, out_t, coefs, hid, hid_t, read):
    s, v, q = mix_orders(mats, mats_t, parts)
    scalars = mixed(out, out_t, product_scalar(coefs, s, v, q)) + residual
    hidden = silu(mixed(hid, hid_t, scalars))
    return jnp.sum(read * hidden, axis=0, keepdims=True)


def radial_forward(w_in_t, mid_stack, basis):
    pre1 = dot_high(w_in_t, basis)
    pre2 = dot_split(mid_stack, silu(pre1))
    return pre1, pre2


def radial_backward(out_back, mid_back, w_in, dw, pre1, pre2):
    dpre2 = dot(out_back, jnp.concatenate([dw, dw], axis=0)) * silu_slope(pre2)
    dpre1 = dot_split(mid_back, dpre2) * silu_slope(pre1)
    return dot_high(w_in, dpre1)


def layer_one_kernel(
    nodes, idx, emb, w_in_t, mid_stack, out_stack, mix, mix_t, outs, outs_t, coefs, border,
    rounded, border_feats, idx_out, offs, f_out, w_out, pre1_out, pre2_out, pooled, y_s,
):
    atoms = rounded.shape[1]
    total = nodes.shape[1]
    slots = idx.shape[1] // atoms
    n = nodes[...]
    hi = n.astype(bf16).astype(f32)
    mid = (n - hi).astype(bf16).astype(f32)
    lo = n - hi - mid
    stack = jnp.concatenate([hi, mid, lo, jnp.zeros_like(lo)], axis=0).astype(bf16)

    def block(b, carry):
        own = nodes[:, pl.ds(pl.multiple_of(b * L, L), L)]
        own2 = jnp.concatenate([own, own], axis=1)

        def gather(c, carry):
            at = pl.ds(pl.multiple_of(b * (L * slots) + c * G, G), G)
            index = idx[:, at]
            got = dot(stack, one_hot_columns(total, index))
            got = got[0:8] + got[8:16] + got[16:24]
            valid = (index >= 0) & (got[4:5] * own2[4:5] > 0.5)
            idx_out[:, at] = jnp.where(valid, index, -1)
            offset = got - own2
            offs[:, at] = offset
            kind = jnp.where(valid, jnp.maximum(got[3:4], 0.0).astype(jnp.int32), -1)
            hot = one_hot_columns(L, kind)
            f_out[:, at] = dot(emb[...], jnp.concatenate([hot, hot], axis=0))
            basis, ys = geometry(offset[0:1], offset[1:2], offset[2:3])
            y_s[:, pl.ds(pl.multiple_of(c * G, G), G)] = jnp.concatenate(ys, axis=0)
            pre1, pre2 = radial_forward(w_in_t[...], mid_stack[...], basis)
            pre1_out[:, at] = pre1
            pre2_out[:, at] = pre2
            w_out[:, at] = dot_split(out_stack[...], silu(pre2))
            return carry

        lax.fori_loop(0, slots * L // G, gather, 0)

        def channels(c, carry):
            row = pl.multiple_of(c * CB, CB)
            acc = [jnp.zeros((CB, L), f32)] * 9
            for s in range(slots):
                at = pl.ds(pl.multiple_of(b * (L * slots) + s * L, L), L)
                f = f_out[pl.ds(row, CB), at]
                w = [w_out[pl.ds(row + p * L, CB), at] * f for p in range(3)]
                acc[0] = acc[0] + w[0]
                for k in range(8):
                    y = y_s[k : k + 1, s * L : (s + 1) * L]
                    acc[1 + k] = acc[1 + k] + (w[1] if k < 3 else w[2]) * y
            for k in range(9):
                pooled[pl.ds(row + k * L, CB), pl.ds(pl.multiple_of(b * L, L), L)] = acc[k] / slots
            return carry

        lax.fori_loop(0, L // CB, channels, 0)
        here = pl.ds(pl.multiple_of(b * L, L), L)
        parts = [pooled[k * L : (k + 1) * L, here] for k in range(9)]
        new = node_one(
            parts, [mix[k] for k in range(3)], [mix_t[k] for k in range(3)],
            [outs[k] for k in range(3)], [outs_t[k] for k in range(3)],
            [coefs[:, k : k + 1] for k in range(5)],
        )
        kind = jnp.maximum(own[3:4], 0.0).astype(jnp.int32)
        hot = one_hot_columns(L, kind)
        new[0] = new[0] + dot(emb[...], jnp.concatenate([hot, hot], axis=0))
        for k in range(9):
            rounded[k * L : (k + 1) * L, here] = new[k].astype(bf16)
        return carry

    lax.fori_loop(0, atoms // L, block, 0)
    border_feats[...] = dot(rounded[...], one_hot_columns(atoms, border[...])).astype(bf16)


def layer_two_kernel(
    rounded, prev, center, nxt, idx, idx_col, offs, occ, w_in, w_in_t, mid_stack, mid_back, out_stack, out_back,
    mix, mix_t, out, out_t, coefs, lin, hid, hid_t, read,
    energy, dlocal, dprev, dcenter, dnext, doffs,
    table, dtable, dres, src, w_s, dw_s, pre1_s, pre2_s, y_s, dy_s, pooled, dpooled,
):
    atoms = energy.shape[1]
    total = table.shape[1]
    slots = idx.shape[1] // atoms
    edges = slots * L
    dtable[...] = jnp.zeros_like(dtable)
    table[:, 0:atoms] = rounded[...]
    table[:, atoms : atoms + 3 * L] = prev[...]
    table[:, atoms + 3 * L : atoms + 6 * L] = center[...]
    table[:, atoms + 6 * L : atoms + 9 * L] = nxt[...]

    def block(b, carry):
        def gather(c, carry):
            at = pl.ds(pl.multiple_of(b * edges + c * G, G), G)
            to = pl.ds(pl.multiple_of(c * G, G), G)
            src[:, to] = dot(table[...], one_hot_columns(total, idx[:, at])).astype(bf16)
            basis, ys = geometry(offs[0:1, at], offs[1:2, at], offs[2:3, at])
            y_s[:, to] = jnp.concatenate(ys, axis=0)
            pre1, pre2 = radial_forward(w_in_t[...], mid_stack[...], basis)
            pre1_s[:, to] = pre1
            pre2_s[:, to] = pre2
            w_s[:, to] = dot_split(out_stack[...], silu(pre2))
            return carry

        lax.fori_loop(0, edges // G, gather, 0)

        def load(row, s):
            at = slice(s * L, (s + 1) * L)
            f = [src[pl.ds(row + k * L, CB), at].astype(f32) for k in range(9)]
            w = [w_s[pl.ds(row + p * L, CB), at] for p in range(7)]
            y = [y_s[k : k + 1, at] for k in range(8)]
            return f, w, y

        def forward(c, carry):
            row = pl.multiple_of(c * CB, CB)
            acc = [jnp.zeros((CB, L), f32)] * 9
            for s in range(slots):
                f, w, y = load(row, s)
                along1 = f[1] * y[0] + f[2] * y[1] + f[3] * y[2]
                along2 = f[4] * y[3] + f[5] * y[4] + f[6] * y[5] + f[7] * y[6] + f[8] * y[7]
                acc[0] = acc[0] + w[0] * f[0] + w[1] * along1 + w[2] * along2
                s1, s2 = w[3] * f[0], w[5] * f[0]
                for k in range(3):
                    acc[1 + k] = acc[1 + k] + s1 * y[k] + w[4] * f[1 + k]
                for k in range(3, 8):
                    acc[1 + k] = acc[1 + k] + s2 * y[k] + w[6] * f[1 + k]
            for k in range(9):
                pooled[pl.ds(row + k * L, CB), :] = acc[k] / slots
            return carry

        lax.fori_loop(0, L // CB, forward, 0)
        here = pl.ds(pl.multiple_of(b * L, L), L)
        mats = [mix[k] for k in range(3)]
        mats_t = [mix_t[k] for k in range(3)]
        cs = [coefs[:, k : k + 1] for k in range(3)]
        occupied = occ[:, here]

        def node(parts, residual):
            return node_two(
                parts, residual, mats, mats_t, out[...], out_t[...], cs,
                hid[...], hid_t[...], read[...],
            )

        residual = table[0:L, here].astype(f32)
        value, pull = jax.vjp(
            node, [pooled[k * L : (k + 1) * L, :] for k in range(9)], residual
        )
        linear = jnp.sum(lin[...] * residual, axis=0, keepdims=True)
        energy[:, here] = (value + linear) * occupied
        dparts, dresidual = pull(occupied)
        for k in range(9):
            dpooled[k * L : (k + 1) * L, :] = dparts[k] / slots
        dy_s[...] = jnp.zeros_like(dy_s)

        def backward(c, carry):
            row = pl.multiple_of(c * CB, CB)
            g = [dpooled[pl.ds(row + k * L, CB), :] for k in range(9)]
            for s in range(slots):
                at = slice(s * L, (s + 1) * L)
                f, w, y = load(row, s)
                dw = [None] * 7
                dw[0] = g[0] * f[0]
                dw[1] = g[0] * (f[1] * y[0] + f[2] * y[1] + f[3] * y[2])
                dw[2] = g[0] * (
                    f[4] * y[3] + f[5] * y[4] + f[6] * y[5] + f[7] * y[6] + f[8] * y[7]
                )
                g1 = g[1] * y[0] + g[2] * y[1] + g[3] * y[2]
                g2 = g[4] * y[3] + g[5] * y[4] + g[6] * y[5] + g[7] * y[6] + g[8] * y[7]
                dw[3] = f[0] * g1
                dw[4] = g[1] * f[1] + g[2] * f[2] + g[3] * f[3]
                dw[5] = f[0] * g2
                dw[6] = g[4] * f[4] + g[5] * f[5] + g[6] * f[6] + g[7] * f[7] + g[8] * f[8]
                for p in range(7):
                    dw_s[pl.ds(row + p * L, CB), at] = dw[p].astype(bf16)
                v0, q0 = w[1] * g[0], w[2] * g[0]
                sv, sq = w[3] * f[0], w[5] * f[0]
                df = w[0] * g[0] + w[3] * g1 + w[5] * g2
                src[pl.ds(row, CB), at] = df.astype(bf16)
                for k in range(8):
                    base = v0 if k < 3 else q0
                    side = sv if k < 3 else sq
                    direct = w[4] if k < 3 else w[6]
                    dy = base * f[1 + k] + side * g[1 + k]
                    dy_s[k * 8 : (k + 1) * 8, at] += dy[0:8] + dy[8:16]
                    df = base * y[k] + direct * g[1 + k]
                    src[pl.ds(row + (1 + k) * L, CB), at] = df.astype(bf16)
            return carry

        lax.fori_loop(0, L // CB, backward, 0)

        def edge_back(c, carry):
            at = pl.ds(pl.multiple_of(b * edges + c * G, G), G)
            to = pl.ds(pl.multiple_of(c * G, G), G)
            dbasis = radial_backward(
                out_back[...], mid_back[...], w_in[...], dw_s[:, to], pre1_s[:, to], pre2_s[:, to]
            )
            dys = tuple(
                jnp.sum(dy_s[k * 8 : (k + 1) * 8, to], axis=0, keepdims=True) for k in range(8)
            )
            _, pull = jax.vjp(geometry, offs[0:1, at], offs[1:2, at], offs[2:3, at])
            dx, dy, dz = pull((dbasis, dys))
            doffs[:, at] = jnp.concatenate([dx, dy, dz, jnp.zeros((5, G), f32)], axis=0)
            return carry

        lax.fori_loop(0, edges // G, edge_back, 0)

        def scatter(t, carry):
            to = pl.ds(pl.multiple_of(t * G, G), G)
            column = idx_col[pl.ds(pl.multiple_of(b * edges, 8), edges), :]
            part = dot(src[...], one_hot_rows(column, t * G, G))

            dtable[:, to] += part
            return carry

        lax.fori_loop(0, total // G, scatter, 0)
        dres[:, here] = dresidual
        return carry

    lax.fori_loop(0, atoms // L, block, 0)
    dlocal[...] = dtable[:, 0:atoms]
    dlocal[0:L, :] += dres[...] + lin[...] * occ[...]
    dprev[...] = dtable[:, atoms : atoms + 3 * L].astype(bf16)
    dcenter[...] = dtable[:, atoms + 3 * L : atoms + 6 * L]
    dnext[...] = dtable[:, atoms + 6 * L : atoms + 9 * L].astype(bf16)


def layer_one_back_kernel(
    dlocal, back, border_col, idx_col, offs, doffs_two, f_in, w_in_edges, pre1_in, pre2_in, pooled,
    w_in, mid_back, out_back, mix, mix_t, outs, outs_t, coefs,
    dpos, dw_s, y_s, dy_s, dh_s, dpooled,
):
    atoms = dlocal.shape[1]
    total = dpos.shape[1]
    slots = offs.shape[1] // atoms
    edges = slots * L
    hot = one_hot_rows(border_col[...], 0, atoms)
    back_hi, back_lo = hi_lo(back[...])
    dh_s[...] = dlocal[...] + dot(back_hi, hot) + dot(back_lo, hot)
    dpos[...] = jnp.zeros_like(dpos)

    def block(b, carry):
        here = pl.ds(pl.multiple_of(b * L, L), L)
        mats = [mix[k] for k in range(3)]
        mats_t = [mix_t[k] for k in range(3)]
        out = [outs[k] for k in range(3)]
        out_t = [outs_t[k] for k in range(3)]
        cs = [coefs[:, k : k + 1] for k in range(5)]
        _, pull = jax.vjp(
            lambda parts: node_one(parts, mats, mats_t, out, out_t, cs),
            [pooled[k * L : (k + 1) * L, here] for k in range(9)],
        )
        (dparts,) = pull([dh_s[k * L : (k + 1) * L, here] for k in range(9)])
        for k in range(9):
            dpooled[k * L : (k + 1) * L, :] = dparts[k] / slots

        def harmonics(c, carry):
            at = pl.ds(pl.multiple_of(b * edges + c * G, G), G)
            _, ys = geometry(offs[0:1, at], offs[1:2, at], offs[2:3, at])
            y_s[:, pl.ds(pl.multiple_of(c * G, G), G)] = jnp.concatenate(ys, axis=0)
            return carry

        lax.fori_loop(0, edges // G, harmonics, 0)
        dy_s[...] = jnp.zeros_like(dy_s)

        def backward(c, carry):
            row = pl.multiple_of(c * CB, CB)
            g = [dpooled[pl.ds(row + k * L, CB), :] for k in range(9)]
            for s in range(slots):
                at = slice(s * L, (s + 1) * L)
                far = pl.ds(pl.multiple_of(b * edges + s * L, L), L)
                f = f_in[pl.ds(row, CB), far]
                y = [y_s[k : k + 1, at] for k in range(8)]
                dw_s[pl.ds(row, CB), at] = (g[0] * f).astype(bf16)
                g1 = g[1] * y[0] + g[2] * y[1] + g[3] * y[2]
                g2 = g[4] * y[3] + g[5] * y[4] + g[6] * y[5] + g[7] * y[6] + g[8] * y[7]
                dw_s[pl.ds(row + L, CB), at] = (f * g1).astype(bf16)
                dw_s[pl.ds(row + 2 * L, CB), at] = (f * g2).astype(bf16)
                w1 = w_in_edges[pl.ds(row + L, CB), far] * f
                w2 = w_in_edges[pl.ds(row + 2 * L, CB), far] * f
                for k in range(8):
                    dy = (w1 if k < 3 else w2) * g[1 + k]
                    dy_s[k * 8 : (k + 1) * 8, at] += dy[0:8] + dy[8:16]
            return carry

        lax.fori_loop(0, L // CB, backward, 0)

        def edge_back(c, own):
            at = pl.ds(pl.multiple_of(b * edges + c * G, G), G)
            to = pl.ds(pl.multiple_of(c * G, G), G)
            dbasis = radial_backward(
                out_back[...], mid_back[...], w_in[...], dw_s[:, to], pre1_in[:, at], pre2_in[:, at]
            )
            dys = tuple(
                jnp.sum(dy_s[k * 8 : (k + 1) * 8, to], axis=0, keepdims=True) for k in range(8)
            )
            _, pull = jax.vjp(geometry, offs[0:1, at], offs[1:2, at], offs[2:3, at])
            dx, dy, dz = pull((dbasis, dys))
            d = jnp.concatenate([dx, dy, dz, jnp.zeros((5, G), f32)], axis=0) + doffs_two[:, at]
            hi = d.astype(bf16).astype(f32)
            both = jnp.concatenate([hi, d - hi], axis=0).astype(bf16)
            column = idx_col[pl.ds(pl.multiple_of(b * edges + c * G, G), G), :]
            part = dot(both, one_hot_rows(column, 0, total))
            dpos[...] += part[0:8] + part[8:16]
            return own + d[:, 0:L] + d[:, L : 2 * L]

        own = lax.fori_loop(0, edges // G, edge_back, jnp.zeros((8, L), f32))
        dpos[:, here] -= own
        return carry

    lax.fori_loop(0, atoms // L, block, 0)


def from_behind(block, axis, distance):
    devices = range(lax.axis_size(axis))
    route = [((i - distance) % len(devices), i) for i in devices]
    return lax.ppermute(block, axis, route)


def parts_of(w):
    hi = lax.reduce_precision(w, 8, 7)
    return hi.astype(bf16), (w - hi).astype(bf16)


def k_stack(w):
    hi, lo = parts_of(w)
    return jnp.concatenate([hi, lo, hi], axis=-1)


def call(kernel, outs, scratch, *args):
    return pl.pallas_call(
        kernel,
        out_shape=[jax.ShapeDtypeStruct(s, d) for s, d in outs],
        scratch_shapes=[pltpu.VMEM(s, d) for s, d in scratch],
        compiler_params=params(),
    )(*args)


def on_device(
    positions, species, dest_key, send_list, send_count, border, neighbours, embedding, radial_in,
    radial_mid, radial_out_one, radial_out_two, mix, mix_out_one, mix_out_two, product_one,
    product_two, read_lin, read_hidden, read_out,
):
    own_coords = positions[0, 0]
    own_kinds = species[0, 0]
    listed = send_list[0, 0]
    border_rows = border[0, 0]
    slot_count = listed.shape[1]
    atoms, slots = neighbours.shape[2:]
    count = border_rows.shape[0]
    edge_total = atoms * slots
    total = atoms + 9 * count
    channels = embedding.shape[1]
    feats = 9 * channels

    packet = jnp.concatenate([own_coords, own_kinds.astype(f32)[None]], axis=0)
    wanted = jnp.concatenate([listed.reshape(-1), border_rows])
    hot = (jnp.arange(own_kinds.shape[0])[:, None] == wanted[None, :]).astype(f32)
    picked = jnp.dot(packet, hot, precision=highest)
    used = jnp.arange(slot_count)[None, :] < send_count[0, 0][:, None]
    used = jnp.concatenate([used.reshape(-1), jnp.ones((count,), bool)])
    picked = jnp.concatenate([picked[:3], jnp.where(used, picked[3], -1.0)[None]], axis=0)
    leave = [picked[:, d * slot_count : (d + 1) * slot_count] for d in range(4)]
    edge_packet = picked[:, 4 * slot_count :]
    up = from_behind(jnp.concatenate([edge_packet, leave[0]], axis=1), "gx", 1)
    down = from_behind(jnp.concatenate([edge_packet, leave[1]], axis=1), "gx", -1)

    def shift(block, axis, amount):
        return block + jnp.zeros((4, 1), f32).at[axis, 0].set(amount)

    triple = jnp.concatenate(
        [shift(up[:, :count], 0, -1.0), edge_packet, shift(down[:, :count], 0, 1.0)], axis=1
    )
    before = from_behind(jnp.concatenate([triple, leave[2]], axis=1), "gy", 1)
    after = from_behind(jnp.concatenate([triple, leave[3]], axis=1), "gy", -1)
    local = jnp.concatenate(
        [
            packet,
            shift(up[:, count:], 0, -1.0),
            shift(down[:, count:], 0, 1.0),
            shift(before[:, 3 * count :], 1, -1.0),
            shift(after[:, 3 * count :], 1, 1.0),
        ],
        axis=1,
    )
    staying = (dest_key[0, 0] == 0).astype(f32)
    occupied = jnp.concatenate([staying, (local[3, staying.shape[0] :] >= 0).astype(f32)])
    everything = jnp.concatenate(
        [local, shift(before[:, : 3 * count], 1, -1.0), triple, shift(after[:, : 3 * count], 1, 1.0)],
        axis=1,
    )
    occupied_all = jnp.concatenate([occupied, jnp.ones((9 * count,), f32)])
    nodes = jnp.concatenate([everything, occupied_all[None], jnp.zeros((3, total), f32)], axis=0)

    index = neighbours[0, 0]
    ghost = index - atoms
    which = ghost // count
    moved = atoms + ((which % 3) * 3 + which // 3) * count + ghost % count
    index = jnp.where(index >= atoms, moved, index)
    index = index.reshape(atoms // L, L, slots).transpose(0, 2, 1).reshape(1, edge_total)

    emb = jnp.pad(embedding, ((0, L - embedding.shape[0]), (0, 0))).T
    emb = jnp.concatenate(parts_of(emb), axis=1)
    w_in_t = jnp.swapaxes(radial_in, 1, 2)
    mid_t = k_stack(jnp.swapaxes(radial_mid, 1, 2))
    mid = k_stack(radial_mid)
    one_t, two_t = k_stack(radial_out_one.T), k_stack(radial_out_two.T)
    one_b = jnp.concatenate(parts_of(radial_out_one), axis=1)
    two_b = jnp.concatenate(parts_of(radial_out_two), axis=1)
    mix_t, mix_k = k_stack(jnp.swapaxes(mix, 2, 3)), k_stack(mix)
    outs_t, outs_k = k_stack(jnp.swapaxes(mix_out_one, 1, 2)), k_stack(mix_out_one)

    hidden = radial_in.shape[2]
    rounded, border_feats, idx, offs, f_e, w_e, pre1, pre2, pooled = call(
        layer_one_kernel,
        [
            ((feats, atoms), bf16), ((feats, count), bf16), ((1, edge_total), jnp.int32),
            ((8, edge_total), f32), ((channels, edge_total), f32), ((3 * channels, edge_total), f32),
            ((hidden, edge_total), f32), ((hidden, edge_total), f32), ((feats, atoms), f32),
        ],
        [((8, slots * L), f32)],
        nodes, index, emb, w_in_t[0], mid_t[0], one_t, mix_k[0], mix_t[0], outs_k, outs_t,
        product_one.T, border_rows[None],
    )
    left = from_behind(border_feats, "gx", 1)
    right = from_behind(border_feats, "gx", -1)
    middle = jnp.concatenate([left, border_feats, right], axis=1)
    prev = from_behind(middle, "gy", 1)
    nxt = from_behind(middle, "gy", -1)
    idx_col = idx.reshape(edge_total, 1)

    energy, dlocal, dprev, dcenter, dnext, doffs = call(
        layer_two_kernel,
        [
            ((1, atoms), f32), ((feats, atoms), f32), ((feats, 3 * count), bf16),
            ((feats, 3 * count), f32), ((feats, 3 * count), bf16), ((8, edge_total), f32),
        ],
        [
            ((feats, total), bf16), ((feats, total), f32), ((channels, atoms), f32),
            ((feats, slots * L), bf16), ((7 * channels, slots * L), f32),
            ((7 * channels, slots * L), bf16), ((hidden, slots * L), f32),
            ((hidden, slots * L), f32), ((8, slots * L), f32), ((64, slots * L), f32),
            ((feats, L), f32), ((feats, L), f32),
        ],
        rounded, prev, middle, nxt, idx, idx_col, offs, occupied[None], radial_in[1], w_in_t[1],
        mid_t[1], mid[1], two_t, two_b, mix_k[1], mix_t[1], k_stack(mix_out_two), k_stack(mix_out_two.T), product_two.T,
        read_lin[:, None], k_stack(read_hidden), k_stack(read_hidden.T), read_out[:, None],
    )
    column = dcenter + from_behind(dprev, "gy", -1).astype(f32)
    column = column + from_behind(dnext, "gy", 1).astype(f32)
    back = column[:, count : 2 * count]
    back = back + from_behind(column[:, :count].astype(bf16), "gx", -1).astype(f32)
    back = back + from_behind(column[:, 2 * count :].astype(bf16), "gx", 1).astype(f32)

    (dpos,) = call(
        layer_one_back_kernel,
        [((8, total), f32)],
        [
            ((3 * channels, slots * L), bf16), ((8, slots * L), f32), ((64, slots * L), f32),
            ((feats, atoms), f32), ((feats, L), f32),
        ],
        dlocal, back, border_rows[:, None], idx_col, offs, doffs, f_e, w_e, pre1, pre2, pooled,
        radial_in[0], mid[0], one_b, mix_k[0], mix_t[0], outs_k, outs_t, product_one.T,
    )
    dpos = dpos[:3]
    column = dpos[:, atoms + 3 * count : atoms + 6 * count]
    column = column + from_behind(dpos[:, atoms : atoms + 3 * count], "gy", -1)
    column = column + from_behind(dpos[:, atoms + 6 * count :], "gy", 1)
    back = column[:, count : 2 * count]
    back = back + from_behind(column[:, :count], "gx", -1)
    back = back + from_behind(column[:, 2 * count :], "gx", 1)
    hot = (border_rows[:, None] == jnp.arange(atoms)[None, :]).astype(f32)
    forces = -(dpos[:, :atoms] + jnp.dot(back, hot, precision=highest))
    return (energy[None], forces[None, None])


def solution(mesh):
    whole = P()
    in_specs = (
        P("gx", "gy", None, None),
        P("gx", "gy", None),
        P("gx", "gy", None),
        P("gx", "gy", None, None),
        P("gx", "gy", None),
        P("gx", "gy", None),
        P("gx", "gy", None, None),
    ) + (whole,) * 13
    out_specs = (P("gx", "gy", None), P("gx", "gy", None, None))
    return jax.shard_map(
        on_device, mesh=mesh, in_specs=in_specs, out_specs=out_specs, check_vma=False
    )
```

```python
import math

import jax
import jax.numpy as jnp
from jax import lax
from jax.experimental import pallas as pl
from jax.experimental.pallas import tpu as pltpu
from jax.sharding import PartitionSpec as P

f32 = jnp.float32
bf16 = jnp.bfloat16
highest = lax.Precision.HIGHEST
CUT = 5.0
L = 128
G = 256
CB = 16
VMEM_LIMIT = 56 * 1024 * 1024


def params():
    return pltpu.CompilerParams(vmem_limit_bytes=VMEM_LIMIT)


def dot(a, b):
    return jnp.dot(a, b, preferred_element_type=f32)


def dot_high(a, b):
    return jnp.dot(a, b, preferred_element_type=f32, precision=highest)


def hi_lo(x):
    hi = x.astype(bf16)
    return hi, (x - hi.astype(f32)).astype(bf16)


def split_stack(x):
    hi, lo = hi_lo(x)
    return jnp.concatenate([hi, hi, lo], axis=0)


def split_stack_small(x):
    hi = x.astype(bf16).astype(f32)
    return jnp.concatenate([hi, hi, x - hi], axis=0).astype(bf16)


def dot_split(stack, x):
    return dot(stack, split_stack(x))


def silu(x):
    return x * jax.nn.sigmoid(x)


def silu_slope(x):
    sig = jax.nn.sigmoid(x)
    return sig * (1.0 + x * (1.0 - sig))


def geometry(ox, oy, oz):
    squared = ox * ox + oy * oy + oz * oz + 1.0
    distance = jnp.sqrt(squared)
    inverse = 1.0 / distance
    ux, uy, uz = ox * inverse, oy * inverse, oz * inverse
    t = distance / CUT
    sixth = t * t * t * t * t * t
    envelope = 1.0 - 28.0 * sixth + 48.0 * sixth * t - 21.0 * sixth * t * t
    orders = (lax.broadcasted_iota(jnp.int32, (8, ox.shape[1]), 0) + 1).astype(f32)
    wave = jnp.sin(orders * (math.pi / CUT) * jnp.broadcast_to(distance, orders.shape))
    scale = math.sqrt(2.0 / CUT) * envelope * inverse
    basis = wave * jnp.broadcast_to(scale, orders.shape)
    r3, r5, r15 = math.sqrt(3.0), math.sqrt(5.0), math.sqrt(15.0)
    harmonics = (
        r3 * ux,
        r3 * uy,
        r3 * uz,
        r15 * ux * uy,
        r15 * uy * uz,
        0.5 * r5 * (2.0 * uz * uz - ux * ux - uy * uy),
        r15 * ux * uz,
        0.5 * r15 * (ux * ux - uy * uy),
    )
    return basis, harmonics


def one_hot_columns(rows, index_row):
    place = lax.broadcasted_iota(jnp.int32, (rows, index_row.shape[1]), 0)
    return jnp.where(place == index_row, 1.0, 0.0).astype(bf16)


def one_hot_rows(index_column, base, columns):
    place = lax.broadcasted_iota(jnp.int32, (index_column.shape[0], columns), 1) + base
    return jnp.where(place == index_column, 1.0, 0.0).astype(bf16)


@jax.custom_vjp
def mixed(w, wt, x):
    return dot_split(wt, x)


def mixed_fwd(w, wt, x):
    return dot_split(wt, x), (w, wt)


def mixed_bwd(saved, g):
    w, wt = saved
    return None, None, dot_split(w, g)


mixed.defvjp(mixed_fwd, mixed_bwd)


def mix_orders(mats, mats_t, parts):
    scalar = mixed(mats[0], mats_t[0], parts[0])
    vector = mixed(mats[1], mats_t[1], jnp.concatenate(parts[1:4], axis=1))
    tensor = mixed(mats[2], mats_t[2], jnp.concatenate(parts[4:9], axis=1))
    return scalar, [vector[:, i * L : (i + 1) * L] for i in range(3)], [
        tensor[:, i * L : (i + 1) * L] for i in range(5)
    ]


def product_scalar(coefs, s, v, q):
    total = s + coefs[0] * s * s
    total = total + coefs[1] * (v[0] * v[0] + v[1] * v[1] + v[2] * v[2])
    return total + coefs[2] * (
        q[0] * q[0] + q[1] * q[1] + q[2] * q[2] + q[3] * q[3] + q[4] * q[4]
    )


def node_one(parts, mats, mats_t, outs, outs_t, coefs):
    s, v, q = mix_orders(mats, mats_t, parts)
    b0 = product_scalar(coefs, s, v, q)
    gate1 = 1.0 + coefs[3] * s
    gate2 = 1.0 + coefs[4] * s
    s, v, q = mix_orders(outs, outs_t, [b0] + [x * gate1 for x in v] + [x * gate2 for x in q])
    return [s] + v + q


def node_two(parts, residual, mats, mats_t, out, out_t, coefs, hid, hid_t, read):
    s, v, q = mix_orders(mats, mats_t, parts)
    scalars = mixed(out, out_t, product_scalar(coefs, s, v, q)) + residual
    hidden = silu(mixed(hid, hid_t, scalars))
    return jnp.sum(read * hidden, axis=0, keepdims=True)


def radial_forward(w_in_t, mid_stack, basis):
    pre1 = dot(w_in_t, split_stack_small(basis))
    pre2 = dot_split(mid_stack, silu(pre1))
    return pre1, pre2


def radial_backward(out_back, mid_back, w_in, dw, pre1, pre2):
    both = dot(out_back, dw)
    half = both.shape[0] // 2
    dpre2 = (both[:half] + both[half:]) * silu_slope(pre2)
    dpre1 = dot_split(mid_back, dpre2) * silu_slope(pre1)
    return dot_split(w_in, dpre1)


def layer_one_kernel(
    nodes, idx, emb, w_in_t, mid_stack, out_stack, mix, mix_t, outs, outs_t, coefs, border,
    rounded, border_feats, idx_out, offs, f_out, w_out, pre1_out, pre2_out, pooled, y_s,
):
    atoms = rounded.shape[1]
    total = nodes.shape[1]
    slots = idx.shape[1] // atoms
    n = nodes[...]
    hi = n.astype(bf16).astype(f32)
    mid = (n - hi).astype(bf16).astype(f32)
    lo = n - hi - mid
    stack = jnp.concatenate([hi, mid, lo, jnp.zeros_like(lo)], axis=0).astype(bf16)

    def block(b, carry):
        own = nodes[:, pl.ds(pl.multiple_of(b * L, L), L)]
        own2 = jnp.concatenate([own, own], axis=1)

        def gather(c, carry):
            at = pl.ds(pl.multiple_of(b * (L * slots) + c * G, G), G)
            index = idx[:, at]
            got = dot(stack, one_hot_columns(total, index))
            got = got[0:8] + got[8:16] + got[16:24]
            valid = (index >= 0) & (got[4:5] * own2[4:5] > 0.5)
            idx_out[:, at] = jnp.where(valid, index, -1)
            offset = got - own2
            offs[:, at] = offset
            kind = jnp.where(valid, jnp.maximum(got[3:4], 0.0).astype(jnp.int32), -1)
            hot = one_hot_columns(L, kind)
            f_out[:, at] = dot(emb[...], jnp.concatenate([hot, hot], axis=0))
            return carry

        lax.fori_loop(0, slots * L // G, gather, 0, unroll=2)
        all_at = pl.ds(pl.multiple_of(b * (L * slots), L), L * slots)
        basis, ys = geometry(offs[0:1, all_at], offs[1:2, all_at], offs[2:3, all_at])
        y_s[...] = jnp.concatenate(ys, axis=0)
        pre1, pre2 = radial_forward(w_in_t[...], mid_stack[...], basis)
        pre1_out[:, all_at] = pre1
        pre2_out[:, all_at] = pre2
        w_out[:, all_at] = dot_split(out_stack[...], silu(pre2))

        def channels(c, carry):
            row = pl.multiple_of(c * CB, CB)
            acc = [jnp.zeros((CB, L), f32)] * 9
            for s in range(slots):
                at = pl.ds(pl.multiple_of(b * (L * slots) + s * L, L), L)
                f = f_out[pl.ds(row, CB), at]
                w = [w_out[pl.ds(row + p * L, CB), at] * f for p in range(3)]
                acc[0] = acc[0] + w[0]
                for k in range(8):
                    y = y_s[k : k + 1, s * L : (s + 1) * L]
                    acc[1 + k] = acc[1 + k] + (w[1] if k < 3 else w[2]) * y
            for k in range(9):
                pooled[pl.ds(row + k * L, CB), pl.ds(pl.multiple_of(b * L, L), L)] = acc[k] / slots
            return carry

        lax.fori_loop(0, L // CB, channels, 0)
        here = pl.ds(pl.multiple_of(b * L, L), L)
        parts = [pooled[k * L : (k + 1) * L, here] for k in range(9)]
        new = node_one(
            parts, [mix[k] for k in range(3)], [mix_t[k] for k in range(3)],
            [outs[k] for k in range(3)], [outs_t[k] for k in range(3)],
            [coefs[:, k : k + 1] for k in range(5)],
        )
        kind = jnp.maximum(own[3:4], 0.0).astype(jnp.int32)
        hot = one_hot_columns(L, kind)
        new[0] = new[0] + dot(emb[...], jnp.concatenate([hot, hot], axis=0))
        for k in range(9):
            rounded[k * L : (k + 1) * L, here] = new[k].astype(bf16)
        return carry

    lax.fori_loop(0, atoms // L, block, 0)
    border_feats[...] = dot(rounded[...], one_hot_columns(atoms, border[...])).astype(bf16)


def radial_two_kernel(offs, w_in_t, mid_stack, h_out, pre1_out, pre2_out, y_out):
    edges = offs.shape[1] // 3

    def block(b, carry):
        at = pl.ds(pl.multiple_of(b * edges, L), edges)
        basis, ys = geometry(offs[0:1, at], offs[1:2, at], offs[2:3, at])
        y_out[:, at] = jnp.concatenate(ys, axis=0)
        pre1, pre2 = radial_forward(w_in_t[...], mid_stack[...], basis)
        pre1_out[:, at] = pre1
        pre2_out[:, at] = pre2
        h_out[:, at] = split_stack(silu(pre2))
        return carry

    lax.fori_loop(0, 3, block, 0)


def radial_two_back_kernel(dw, dy, pre1, pre2, offs, w_in, mid_back, out_back, doffs):
    blocks, _, edges = dw.shape

    def block(b, carry):
        at = pl.ds(pl.multiple_of(b * edges, L), edges)
        dbasis = radial_backward(
            out_back[...], mid_back[...], w_in[...], dw[b], pre1[:, at], pre2[:, at]
        )
        dys = tuple(
            jnp.sum(dy[k * 8 : (k + 1) * 8, at], axis=0, keepdims=True) for k in range(8)
        )
        _, pull = jax.vjp(geometry, offs[0:1, at], offs[1:2, at], offs[2:3, at])
        dx, dyy, dz = pull((dbasis, dys))
        doffs[:, at] = jnp.concatenate([dx, dyy, dz, jnp.zeros((5, edges), f32)], axis=0)
        return carry

    lax.fori_loop(0, blocks, block, 0)


def layer_two_kernel(
    rounded, own_prev, side_prev, side, own_next, side_next, idx, idx_col, h_in, y_in, occ,
    out_stack, mix, mix_t, out, out_t, coefs, lin, hid, hid_t, read,
    energy, dlocal, down_prev, dside_prev, dside, down_next, dside_next, dy_out, dw_out,
    table, dtable, dres, src, w_s, dw_s, pooled, dpooled, dw_sem,
):
    atoms = energy.shape[1]
    total = table.shape[1]
    slots = idx.shape[1] // atoms
    edges = slots * L
    first, second, third = atoms, atoms + 3 * L, atoms + 6 * L
    dtable[...] = jnp.zeros_like(dtable)
    table[:, 0:atoms] = rounded[...]
    table[:, first : first + L] = own_prev[...]
    table[:, first + L : second] = side_prev[...]
    table[:, second : second + L] = jnp.zeros((9 * L, L), bf16)
    table[:, second + L : third] = side[...]
    table[:, third : third + L] = own_next[...]
    table[:, third + L : third + 3 * L] = side_next[...]

    def block(b, carry):
        def gather(c, carry):
            at = pl.ds(pl.multiple_of(b * edges + c * G, G), G)
            to = pl.ds(pl.multiple_of(c * G, G), G)
            src[:, to] = dot(table[...], one_hot_columns(total, idx[:, at])).astype(bf16)
            w_s[:, to] = dot(out_stack[...], h_in[:, at])
            return carry

        lax.fori_loop(0, edges // G, gather, 0)

        def load(row, s):
            at = slice(s * L, (s + 1) * L)
            f = [src[pl.ds(row + k * L, CB), at].astype(f32) for k in range(9)]
            w = [w_s[pl.ds(row + p * L, CB), at] for p in range(7)]
            far = pl.ds(pl.multiple_of(b * edges + s * L, L), L)
            y = [y_in[k : k + 1, far] for k in range(8)]
            return f, w, y

        def forward(c, carry):
            row = pl.multiple_of(c * CB, CB)
            acc = [jnp.zeros((CB, L), f32)] * 9
            for s in range(slots):
                f, w, y = load(row, s)
                along1 = f[1] * y[0] + f[2] * y[1] + f[3] * y[2]
                along2 = f[4] * y[3] + f[5] * y[4] + f[6] * y[5] + f[7] * y[6] + f[8] * y[7]
                acc[0] = acc[0] + w[0] * f[0] + w[1] * along1 + w[2] * along2
                s1, s2 = w[3] * f[0], w[5] * f[0]
                for k in range(3):
                    acc[1 + k] = acc[1 + k] + s1 * y[k] + w[4] * f[1 + k]
                for k in range(3, 8):
                    acc[1 + k] = acc[1 + k] + s2 * y[k] + w[6] * f[1 + k]
            for k in range(9):
                pooled[pl.ds(row + k * L, CB), :] = acc[k] / slots
            return carry

        lax.fori_loop(0, L // CB, forward, 0)
        here = pl.ds(pl.multiple_of(b * L, L), L)
        mats = [mix[k] for k in range(3)]
        mats_t = [mix_t[k] for k in range(3)]
        cs = [coefs[:, k : k + 1] for k in range(3)]
        occupied = occ[:, here]

        def node(parts, residual):
            return node_two(
                parts, residual, mats, mats_t, out[...], out_t[...], cs,
                hid[...], hid_t[...], read[...],
            )

        residual = table[0:L, here].astype(f32)
        value, pull = jax.vjp(
            node, [pooled[k * L : (k + 1) * L, :] for k in range(9)], residual
        )
        linear = jnp.sum(lin[...] * residual, axis=0, keepdims=True)
        energy[:, here] = (value + linear) * occupied
        dparts, dresidual = pull(occupied)
        for k in range(9):
            dpooled[k * L : (k + 1) * L, :] = dparts[k] / slots
        mine = pl.ds(pl.multiple_of(b * edges, L), edges)
        dy_out[:, mine] = jnp.zeros((64, edges), f32)

        def backward(c, carry):
            row = pl.multiple_of(c * CB, CB)
            g = [dpooled[pl.ds(row + k * L, CB), :] for k in range(9)]
            for s in range(slots):
                at = slice(s * L, (s + 1) * L)
                far = pl.ds(pl.multiple_of(b * edges + s * L, L), L)
                f, w, y = load(row, s)
                dw = [None] * 7
                dw[0] = g[0] * f[0]
                dw[1] = g[0] * (f[1] * y[0] + f[2] * y[1] + f[3] * y[2])
                dw[2] = g[0] * (
                    f[4] * y[3] + f[5] * y[4] + f[6] * y[5] + f[7] * y[6] + f[8] * y[7]
                )
                g1 = g[1] * y[0] + g[2] * y[1] + g[3] * y[2]
                g2 = g[4] * y[3] + g[5] * y[4] + g[6] * y[5] + g[7] * y[6] + g[8] * y[7]
                dw[3] = f[0] * g1
                dw[4] = g[1] * f[1] + g[2] * f[2] + g[3] * f[3]
                dw[5] = f[0] * g2
                dw[6] = g[4] * f[4] + g[5] * f[5] + g[6] * f[6] + g[7] * f[7] + g[8] * f[8]
                for p in range(7):
                    dw_s[pl.ds(row + p * L, CB), at] = dw[p].astype(bf16)
                v0, q0 = w[1] * g[0], w[2] * g[0]
                sv, sq = w[3] * f[0], w[5] * f[0]
                df = w[0] * g[0] + w[3] * g1 + w[5] * g2
                src[pl.ds(row, CB), at] = df.astype(bf16)
                for k in range(8):
                    base = v0 if k < 3 else q0
                    side = sv if k < 3 else sq
                    direct = w[4] if k < 3 else w[6]
                    dy = base * f[1 + k] + side * g[1 + k]
                    dy_out[k * 8 : (k + 1) * 8, far] += dy[0:8] + dy[8:16]
                    df = base * y[k] + direct * g[1 + k]
                    src[pl.ds(row + (1 + k) * L, CB), at] = df.astype(bf16)
            return carry

        lax.fori_loop(0, L // CB, backward, 0)

        keep = pltpu.make_async_copy(dw_s, dw_out.at[b], dw_sem)
        keep.start()

        def scatter(t, carry):
            to = pl.ds(pl.multiple_of(t * G, G), G)
            column = idx_col[pl.ds(pl.multiple_of(b * edges, 8), edges), :]
            part = dot(src[...], one_hot_rows(column, t * G, G))

            dtable[:, to] += part
            return carry

        lax.fori_loop(0, total // G, scatter, 0)
        keep.wait()
        dres[:, here] = dresidual
        return carry

    lax.fori_loop(0, atoms // L, block, 0)
    dlocal[...] = dtable[:, 0:atoms]
    dlocal[0:L, :] += dres[...] + lin[...] * occ[...]
    down_prev[...] = dtable[:, first : first + L].astype(bf16)
    dside_prev[...] = dtable[:, first + L : second].astype(bf16)
    dside[...] = dtable[:, second + L : third]
    down_next[...] = dtable[:, third : third + L].astype(bf16)
    dside_next[...] = dtable[:, third + L : third + 3 * L].astype(bf16)


def layer_one_back_kernel(
    dlocal, back_a, back_b, back_c, back_d, border_col, idx_col, offs, doffs_two, f_in, w_in_edges, pre1_in, pre2_in, pooled,
    w_in, mid_back, out_back, mix, mix_t, outs, outs_t, coefs,
    dpos, dw_s, y_s, dy_s, dh_s, dpooled, d_s,
):
    atoms = dlocal.shape[1]
    total = dpos.shape[1]
    slots = offs.shape[1] // atoms
    edges = slots * L
    hot = one_hot_rows(border_col[...], 0, atoms)
    back = (back_a[...].astype(f32) + back_b[...].astype(f32)) + (
        back_c[...].astype(f32) + back_d[...].astype(f32)
    )
    back_hi, back_lo = hi_lo(back)
    dh_s[...] = dlocal[...] + dot(back_hi, hot) + dot(back_lo, hot)
    dpos[...] = jnp.zeros_like(dpos)

    def block(b, carry):
        here = pl.ds(pl.multiple_of(b * L, L), L)
        mats = [mix[k] for k in range(3)]
        mats_t = [mix_t[k] for k in range(3)]
        out = [outs[k] for k in range(3)]
        out_t = [outs_t[k] for k in range(3)]
        cs = [coefs[:, k : k + 1] for k in range(5)]
        _, pull = jax.vjp(
            lambda parts: node_one(parts, mats, mats_t, out, out_t, cs),
            [pooled[k * L : (k + 1) * L, here] for k in range(9)],
        )
        (dparts,) = pull([dh_s[k * L : (k + 1) * L, here] for k in range(9)])
        for k in range(9):
            dpooled[k * L : (k + 1) * L, :] = dparts[k] / slots

        mine = pl.ds(pl.multiple_of(b * edges, L), edges)
        _, ys = geometry(offs[0:1, mine], offs[1:2, mine], offs[2:3, mine])
        y_s[...] = jnp.concatenate(ys, axis=0)
        dy_s[...] = jnp.zeros_like(dy_s)

        def backward(c, carry):
            row = pl.multiple_of(c * CB, CB)
            g = [dpooled[pl.ds(row + k * L, CB), :] for k in range(9)]
            for s in range(slots):
                at = slice(s * L, (s + 1) * L)
                far = pl.ds(pl.multiple_of(b * edges + s * L, L), L)
                f = f_in[pl.ds(row, CB), far]
                y = [y_s[k : k + 1, at] for k in range(8)]
                dw_s[pl.ds(row, CB), at] = (g[0] * f).astype(bf16)
                g1 = g[1] * y[0] + g[2] * y[1] + g[3] * y[2]
                g2 = g[4] * y[3] + g[5] * y[4] + g[6] * y[5] + g[7] * y[6] + g[8] * y[7]
                dw_s[pl.ds(row + L, CB), at] = (f * g1).astype(bf16)
                dw_s[pl.ds(row + 2 * L, CB), at] = (f * g2).astype(bf16)
                w1 = w_in_edges[pl.ds(row + L, CB), far] * f
                w2 = w_in_edges[pl.ds(row + 2 * L, CB), far] * f
                for k in range(8):
                    dy = (w1 if k < 3 else w2) * g[1 + k]
                    dy_s[k * 8 : (k + 1) * 8, at] += dy[0:8] + dy[8:16]
            return carry

        lax.fori_loop(0, L // CB, backward, 0)

        dbasis = radial_backward(
            out_back[...], mid_back[...], w_in[...], dw_s[...], pre1_in[:, mine], pre2_in[:, mine]
        )
        dys = tuple(
            jnp.sum(dy_s[k * 8 : (k + 1) * 8, :], axis=0, keepdims=True) for k in range(8)
        )
        _, pull_again = jax.vjp(geometry, offs[0:1, mine], offs[1:2, mine], offs[2:3, mine])
        dx, dy, dz = pull_again((dbasis, dys))
        d = jnp.concatenate([dx, dy, dz, jnp.zeros((5, edges), f32)], axis=0) + doffs_two[:, mine]
        hi = d.astype(bf16).astype(f32)
        d_s[...] = jnp.concatenate([hi, d - hi], axis=0).astype(bf16)
        own = d[:, 0:L]
        for s in range(1, slots):
            own = own + d[:, s * L : (s + 1) * L]

        def scatter(t, carry):
            to = pl.ds(pl.multiple_of(t * G, G), G)
            column = idx_col[pl.ds(pl.multiple_of(b * edges, 8), edges), :]
            part = dot(d_s[...], one_hot_rows(column, t * G, G))
            dpos[:, to] += part[0:8] + part[8:16]
            return carry

        lax.fori_loop(0, total // G, scatter, 0)
        dpos[:, here] -= own
        return carry

    lax.fori_loop(0, atoms // L, block, 0)


def from_behind(block, axis, distance):
    devices = range(lax.axis_size(axis))
    route = [((i - distance) % len(devices), i) for i in devices]
    return lax.ppermute(block, axis, route)


def parts_of(w):
    hi = lax.reduce_precision(w, 8, 7)
    return hi.astype(bf16), (w - hi).astype(bf16)


def k_stack(w):
    hi, lo = parts_of(w)
    return jnp.concatenate([hi, lo, hi], axis=-1)


def call(kernel, outs, scratch, *args, flops=0, any_outs=()):
    cost = None
    if flops:
        cost = pl.CostEstimate(flops=flops, bytes_accessed=16 * 1024 * 1024, transcendentals=0)
    specs = [
        pl.BlockSpec(memory_space=pl.ANY if i in any_outs else pltpu.VMEM)
        for i in range(len(outs))
    ]
    return pl.pallas_call(
        kernel,
        out_shape=[jax.ShapeDtypeStruct(s, d) for s, d in outs],
        out_specs=specs,
        scratch_shapes=[pltpu.VMEM(s, d) for s, d in scratch]
        + [pltpu.SemaphoreType.DMA(())] * len(any_outs),
        cost_estimate=cost,
        compiler_params=params(),
    )(*args)


def on_device(
    positions, species, dest_key, send_list, send_count, border, neighbours, embedding, radial_in,
    radial_mid, radial_out_one, radial_out_two, mix, mix_out_one, mix_out_two, product_one,
    product_two, read_lin, read_hidden, read_out,
):
    own_coords = positions[0, 0]
    own_kinds = species[0, 0]
    listed = send_list[0, 0]
    border_rows = border[0, 0]
    slot_count = listed.shape[1]
    atoms, slots = neighbours.shape[2:]
    count = border_rows.shape[0]
    edge_total = atoms * slots
    total = atoms + 9 * count
    channels = embedding.shape[1]
    feats = 9 * channels

    packet = jnp.concatenate([own_coords, own_kinds.astype(f32)[None]], axis=0)
    wanted = jnp.concatenate([listed.reshape(-1), border_rows])
    hot = (jnp.arange(own_kinds.shape[0])[:, None] == wanted[None, :]).astype(f32)
    picked = jnp.dot(packet, hot, precision=highest)
    used = jnp.arange(slot_count)[None, :] < send_count[0, 0][:, None]
    used = jnp.concatenate([used.reshape(-1), jnp.ones((count,), bool)])
    picked = jnp.concatenate([picked[:3], jnp.where(used, picked[3], -1.0)[None]], axis=0)
    leave = [picked[:, d * slot_count : (d + 1) * slot_count] for d in range(4)]
    edge_packet = picked[:, 4 * slot_count :]
    up = from_behind(jnp.concatenate([edge_packet, leave[0]], axis=1), "gx", 1)
    down = from_behind(jnp.concatenate([edge_packet, leave[1]], axis=1), "gx", -1)

    def shift(block, axis, amount):
        return block + jnp.zeros((4, 1), f32).at[axis, 0].set(amount)

    triple = jnp.concatenate(
        [edge_packet, shift(up[:, :count], 0, -1.0), shift(down[:, :count], 0, 1.0)], axis=1
    )
    before = from_behind(jnp.concatenate([triple, leave[2]], axis=1), "gy", 1)
    after = from_behind(jnp.concatenate([triple, leave[3]], axis=1), "gy", -1)
    local = jnp.concatenate(
        [
            packet,
            shift(up[:, count:], 0, -1.0),
            shift(down[:, count:], 0, 1.0),
            shift(before[:, 3 * count :], 1, -1.0),
            shift(after[:, 3 * count :], 1, 1.0),
        ],
        axis=1,
    )
    staying = (dest_key[0, 0] == 0).astype(f32)
    occupied = jnp.concatenate([staying, (local[3, staying.shape[0] :] >= 0).astype(f32)])
    everything = jnp.concatenate(
        [local, shift(before[:, : 3 * count], 1, -1.0), triple, shift(after[:, : 3 * count], 1, 1.0)],
        axis=1,
    )
    occupied_all = jnp.concatenate([occupied, jnp.ones((9 * count,), f32)])
    nodes = jnp.concatenate([everything, occupied_all[None], jnp.zeros((3, total), f32)], axis=0)

    index = neighbours[0, 0]
    ghost = index - atoms
    which = ghost // count
    across = which // 3
    across = jnp.where(across == 1, 0, jnp.where(across == 0, 1, 2))
    moved = atoms + ((which % 3) * 3 + across) * count + ghost % count
    index = jnp.where(index >= atoms, moved, index)
    index = index.reshape(atoms // L, L, slots).transpose(0, 2, 1).reshape(1, edge_total)

    emb = jnp.pad(embedding, ((0, L - embedding.shape[0]), (0, 0))).T
    emb = jnp.concatenate(parts_of(emb), axis=1)
    mix_t = k_stack(jnp.swapaxes(mix[0], 1, 2))
    outs_t = k_stack(jnp.swapaxes(mix_out_one, 1, 2))
    one_coefs = product_one.T
    hidden = radial_in.shape[2]
    rounded, border_feats, idx, offs, f_e, w_e, pre1, pre2, pooled = call(
        layer_one_kernel,
        [
            ((feats, atoms), bf16), ((feats, count), bf16), ((1, edge_total), jnp.int32),
            ((8, edge_total), f32), ((channels, edge_total), f32), ((3 * channels, edge_total), f32),
            ((hidden, edge_total), f32), ((hidden, edge_total), f32), ((feats, atoms), f32),
        ],
        [((8, slots * L), f32)],
        nodes, index, emb, k_stack(radial_in[0].T), k_stack(radial_mid[0].T),
        k_stack(radial_out_one.T), mix_t, mix_t, outs_t, outs_t, one_coefs, border_rows[None],
    )
    later = lax.optimization_barrier(
        (border_feats, radial_in, radial_mid, radial_out_one, radial_out_two, mix, mix_out_one,
         mix_out_two, product_two, read_lin, read_hidden, read_out)
    )
    (border_feats, radial_in, radial_mid, radial_out_one, radial_out_two, mix, mix_out_one,
     mix_out_two, product_two, read_lin, read_hidden, read_out) = later
    left = from_behind(border_feats, "gx", 1)
    right = from_behind(border_feats, "gx", -1)
    own_prev = from_behind(border_feats, "gy", 1)
    own_next = from_behind(border_feats, "gy", -1)
    side = jnp.concatenate([left, right], axis=1)
    side_prev = from_behind(side, "gy", 1)
    side_next = from_behind(side, "gy", -1)
    idx_col = idx.reshape(edge_total, 1)

    h_two, pre1_two, pre2_two, y_two = call(
        radial_two_kernel,
        [
            ((3 * hidden, edge_total), bf16), ((hidden, edge_total), f32),
            ((hidden, edge_total), f32), ((8, edge_total), f32),
        ],
        [],
        offs, k_stack(radial_in[1].T), k_stack(radial_mid[1].T), flops=10**10,
    )

    two = ((feats, 2 * count), bf16)
    one = ((feats, count), bf16)
    energy, dlocal, down_prev, dside_prev, dside, down_next, dside_next, dy_two, dw_two = call(
        layer_two_kernel,
        [
            ((1, atoms), f32), ((feats, atoms), f32), one, two, ((feats, 2 * count), f32), one, two,
            ((64, edge_total), f32), ((atoms // L, 7 * channels, slots * L), bf16),
        ],
        [
            ((feats, total), bf16), ((feats, total), f32), ((channels, atoms), f32),
            ((feats, slots * L), bf16), ((7 * channels, slots * L), f32),
            ((7 * channels, slots * L), bf16), ((feats, L), f32), ((feats, L), f32),
        ],
        rounded, own_prev, side_prev, side, own_next, side_next, idx, idx_col, h_two, y_two,
        occupied[None], k_stack(radial_out_two.T), k_stack(mix[1]),
        k_stack(jnp.swapaxes(mix[1], 1, 2)), k_stack(mix_out_two), k_stack(mix_out_two.T),
        product_two.T, read_lin[:, None], k_stack(read_hidden), k_stack(read_hidden.T),
        read_out[:, None], flops=10**11, any_outs=(8,),
    )
    side_a = from_behind(dside_prev, "gy", -1)
    side_b = from_behind(dside_next, "gy", 1)
    side_a, side_b, down_prev, down_next = lax.optimization_barrier(
        (side_a, side_b, down_prev, down_next)
    )
    back_a = from_behind(down_prev, "gy", -1)
    back_b = from_behind(down_next, "gy", 1)
    dside = (dside + side_a.astype(f32) + side_b.astype(f32)).astype(bf16)
    back_c = from_behind(dside[:, :count], "gx", -1)
    back_d = from_behind(dside[:, count:], "gx", 1)
    (doffs,) = call(
        radial_two_back_kernel, [((8, edge_total), f32)], [],
        dw_two, dy_two, pre1_two, pre2_two, offs, k_stack(radial_in[1]), k_stack(radial_mid[1]),
        jnp.concatenate(parts_of(radial_out_two), axis=0), flops=10**10,
    )

    (dpos,) = call(
        layer_one_back_kernel,
        [((8, total), f32)],
        [
            ((3 * channels, slots * L), bf16), ((8, slots * L), f32), ((64, slots * L), f32),
            ((feats, atoms), f32), ((feats, L), f32), ((16, slots * L), bf16),
        ],
        dlocal, back_a, back_b, back_c, back_d, border_rows[:, None], idx_col, offs, doffs, f_e, w_e,
        pre1, pre2, pooled, k_stack(radial_in[0]), k_stack(radial_mid[0]),
        jnp.concatenate(parts_of(radial_out_one), axis=0), k_stack(mix[0]), mix_t,
        k_stack(mix_out_one), outs_t, one_coefs,
    )
    dpos = dpos[:3]
    column = dpos[:, atoms + 3 * count : atoms + 6 * count]
    column = column + from_behind(dpos[:, atoms : atoms + 3 * count], "gy", -1)
    column = column + from_behind(dpos[:, atoms + 6 * count :], "gy", 1)
    back = column[:, :count]
    back = back + from_behind(column[:, count : 2 * count], "gx", -1)
    back = back + from_behind(column[:, 2 * count :], "gx", 1)
    hot = (border_rows[:, None] == jnp.arange(atoms)[None, :]).astype(f32)
    forces = -(dpos[:, :atoms] + jnp.dot(back, hot, precision=highest))
    return (energy[None], forces[None, None])


def solution(mesh):
    whole = P()
    in_specs = (
        P("gx", "gy", None, None),
        P("gx", "gy", None),
        P("gx", "gy", None),
        P("gx", "gy", None, None),
        P("gx", "gy", None),
        P("gx", "gy", None),
        P("gx", "gy", None, None),
    ) + (whole,) * 13
    out_specs = (P("gx", "gy", None), P("gx", "gy", None, None))
    return jax.shard_map(
        on_device, mesh=mesh, in_specs=in_specs, out_specs=out_specs, check_vma=False
    )
```

```python
import functools
import math

import jax
import jax.numpy as jnp
from jax import lax
from jax.experimental import pallas as pl
from jax.experimental.pallas import tpu as pltpu
from jax.sharding import PartitionSpec as P

f32 = jnp.float32
bf16 = jnp.bfloat16
CUT = 5.0
L = 128
G = 256
CB = 16
VMEM_LIMIT = 56 * 1024 * 1024


MESH = pl.DeviceIdType.MESH
AROUND = [(a - 1, b - 1) for a in range(3) for b in range(3) if (a, b) != (1, 1)]
ORDER = sorted(range(8), key=lambda q: -abs(AROUND[q][1]))


def cell(grid, da, db):
    x, y = lax.axis_index("gx"), lax.axis_index("gy")
    return (lax.rem(x + da + grid[0], grid[0]), lax.rem(y + db + grid[1], grid[1]))


def greet(grid):
    barrier = pltpu.get_barrier_semaphore()
    for da, db in AROUND:
        pl.semaphore_signal(barrier, inc=1, device_id=cell(grid, da, db), device_id_type=MESH)
    pl.semaphore_wait(barrier, 8)


def send_around(grid, sign, source, target, sends, recvs):
    copies = []
    for q in ORDER:
        da, db = AROUND[q]
        copy = pltpu.make_async_remote_copy(
            src_ref=source(q),
            dst_ref=target.at[q],
            send_sem=sends.at[q],
            recv_sem=recvs.at[q],
            device_id=cell(grid, sign * da, sign * db),
            device_id_type=MESH,
        )
        copy.start()
        copies.append(copy)
    return copies


def three_parts(x):
    hi = x.astype(bf16).astype(f32)
    mid = (x - hi).astype(bf16).astype(f32)
    return jnp.concatenate([hi, mid, x - hi - mid, jnp.zeros_like(x)], axis=0).astype(bf16)


def exact_pick(x, hot):
    got = dot(three_parts(x), hot)
    return got[0:8] + got[8:16] + got[16:24]


def dot(a, b):
    return jnp.dot(a, b, preferred_element_type=f32)


def hi_lo(x):
    hi = x.astype(bf16)
    return hi, (x - hi.astype(f32)).astype(bf16)


def split_stack(x):
    hi, lo = hi_lo(x)
    return jnp.concatenate([hi, hi, lo], axis=0)


def split_stack_small(x):
    hi = x.astype(bf16).astype(f32)
    return jnp.concatenate([hi, hi, x - hi], axis=0).astype(bf16)


def rows_stack(w):
    if w.shape[0] % 16:
        hi = w.astype(bf16).astype(f32)
        return jnp.concatenate([hi, w - hi, hi], axis=0).astype(bf16)
    hi, lo = hi_lo(w)
    return jnp.concatenate([hi, lo, hi], axis=0)


def lanes_stack(w):
    hi, lo = hi_lo(w)
    return jnp.concatenate([hi, lo, hi], axis=1)


def dot_rows(stack, x_stack):
    return lax.dot_general(
        stack, x_stack, (((0,), (0,)), ((), ())), preferred_element_type=f32
    )


def dot_back(w, x):
    w_hi, w_lo = hi_lo(w)
    x_hi, x_lo = hi_lo(x)
    return dot(w_hi, x_hi) + dot(w_lo, x_hi) + dot(w_hi, x_lo)


def column_of(row):
    size = row.shape[1]
    down = lax.broadcasted_iota(jnp.int32, (size, size), 0)
    along = lax.broadcasted_iota(jnp.int32, (size, size), 1)
    return jnp.sum(jnp.where(down == along, row, 0.0), axis=1, keepdims=True)


def row_of(column):
    size = column.shape[0]
    down = lax.broadcasted_iota(jnp.int32, (size, size), 0)
    along = lax.broadcasted_iota(jnp.int32, (size, size), 1)
    return jnp.sum(jnp.where(down == along, column, 0.0), axis=0, keepdims=True)


def silu(x):
    return x * jax.nn.sigmoid(x)


def silu_slope(x):
    sig = jax.nn.sigmoid(x)
    return sig * (1.0 + x * (1.0 - sig))


def geometry(ox, oy, oz):
    squared = ox * ox + oy * oy + oz * oz + 1.0
    distance = jnp.sqrt(squared)
    inverse = 1.0 / distance
    ux, uy, uz = ox * inverse, oy * inverse, oz * inverse
    t = distance / CUT
    sixth = t * t * t * t * t * t
    envelope = 1.0 - 28.0 * sixth + 48.0 * sixth * t - 21.0 * sixth * t * t
    orders = (lax.broadcasted_iota(jnp.int32, (8, ox.shape[1]), 0) + 1).astype(f32)
    wave = jnp.sin(orders * (math.pi / CUT) * jnp.broadcast_to(distance, orders.shape))
    scale = math.sqrt(2.0 / CUT) * envelope * inverse
    basis = wave * jnp.broadcast_to(scale, orders.shape)
    r3, r5, r15 = math.sqrt(3.0), math.sqrt(5.0), math.sqrt(15.0)
    harmonics = (
        r3 * ux,
        r3 * uy,
        r3 * uz,
        r15 * ux * uy,
        r15 * uy * uz,
        0.5 * r5 * (2.0 * uz * uz - ux * ux - uy * uy),
        r15 * ux * uz,
        0.5 * r15 * (ux * ux - uy * uy),
    )
    return basis, harmonics


def one_hot_columns(rows, index_row):
    place = lax.broadcasted_iota(jnp.int32, (rows, index_row.shape[1]), 0)
    return jnp.where(place == index_row, 1.0, 0.0).astype(bf16)


def one_hot_rows(index_column, base, columns):
    place = lax.broadcasted_iota(jnp.int32, (index_column.shape[0], columns), 1) + base
    return jnp.where(place == index_column, 1.0, 0.0).astype(bf16)


@jax.custom_vjp
def mixed(w, x):
    return dot_rows(w[0], split_stack(x))


def mixed_fwd(w, x):
    return mixed(w, x), w


def mixed_bwd(w, g):
    if w[1].shape[1] % L:
        return None, dot_back(w[1], g)
    return None, dot(w[1], split_stack(g))


mixed.defvjp(mixed_fwd, mixed_bwd)


def both_ways(w):
    return rows_stack(w), lanes_stack(w)


def mix_orders(mats, parts):
    scalar = mixed(mats[0], parts[0])
    vector = mixed(mats[1], jnp.concatenate(parts[1:4], axis=1))
    tensor = mixed(mats[2], jnp.concatenate(parts[4:9], axis=1))
    return scalar, [vector[:, i * L : (i + 1) * L] for i in range(3)], [
        tensor[:, i * L : (i + 1) * L] for i in range(5)
    ]


def product_scalar(coefs, s, v, q):
    total = s + coefs[0] * s * s
    total = total + coefs[1] * (v[0] * v[0] + v[1] * v[1] + v[2] * v[2])
    return total + coefs[2] * (
        q[0] * q[0] + q[1] * q[1] + q[2] * q[2] + q[3] * q[3] + q[4] * q[4]
    )


def node_one(parts, mats, outs, coefs):
    s, v, q = mix_orders(mats, parts)
    b0 = product_scalar(coefs, s, v, q)
    gate1 = 1.0 + coefs[3] * s
    gate2 = 1.0 + coefs[4] * s
    s, v, q = mix_orders(outs, [b0] + [x * gate1 for x in v] + [x * gate2 for x in q])
    return [s] + v + q


def node_two(parts, residual, mats, out, coefs, hid, read):
    s, v, q = mix_orders(mats, parts)
    scalars = mixed(out, product_scalar(coefs, s, v, q)) + residual
    hidden = silu(mixed(hid, scalars))
    return jnp.sum(read * hidden, axis=0, keepdims=True)


def radial_forward(w_in, w_mid, basis):
    pre1 = dot_rows(rows_stack(w_in), split_stack_small(basis))
    pre2 = dot_rows(rows_stack(w_mid), split_stack(silu(pre1)))
    return pre1, pre2


def radial_backward(w_out, w_mid, w_in, dw, pre1, pre2):
    both = dot(jnp.concatenate(hi_lo(w_out), axis=0), dw)
    half = both.shape[0] // 2
    dpre2 = (both[:half] + both[half:]) * silu_slope(pre2)
    dpre1 = dot_back(w_mid, dpre2) * silu_slope(pre1)
    return dot_back(w_in, dpre1)


def layer_one_kernel(
    nodes, idx, emb, w_in, w_mid, w_out, mix, out_mix, coefs, border,
    rounded, border_feats, idx_out, offs, f_out, w_edges, pre1_out, pre2_out, pooled, y_s, emb_s,
):
    atoms = rounded.shape[1]
    total = nodes.shape[1]
    slots = idx.shape[1] // atoms
    stack = three_parts(nodes[...])
    elements = emb_s.shape[0]
    emb_s[...] = jnp.zeros_like(emb_s)
    emb_s[0 : emb.shape[0], :] = emb[...]
    emb_stack = jnp.concatenate(hi_lo(emb_s[...]), axis=0)
    out_stack = rows_stack(w_out[...])
    mats = [both_ways(mix[0, k]) for k in range(3)]
    outs = [both_ways(out_mix[k]) for k in range(3)]
    cs = [column_of(coefs[k : k + 1, :]) for k in range(5)]

    def block(b, carry):
        own = nodes[:, pl.ds(pl.multiple_of(b * L, L), L)]
        own2 = jnp.concatenate([own, own], axis=1)

        def gather(c, carry):
            at = pl.ds(pl.multiple_of(b * (L * slots) + c * G, G), G)
            index = idx[:, at]
            got = dot(stack, one_hot_columns(total, index))
            got = got[0:8] + got[8:16] + got[16:24]
            valid = (index >= 0) & (got[4:5] * own2[4:5] > 0.5)
            idx_out[:, at] = jnp.where(valid, index, -1)
            offset = got - own2
            offs[:, at] = offset
            kind = jnp.where(valid, jnp.maximum(got[3:4], 0.0).astype(jnp.int32), -1)
            hot = one_hot_columns(elements, kind)
            f_out[:, at] = dot_rows(emb_stack, jnp.concatenate([hot, hot], axis=0))
            return carry

        lax.fori_loop(0, slots * L // G, gather, 0, unroll=2)
        all_at = pl.ds(pl.multiple_of(b * (L * slots), L), L * slots)
        basis, ys = geometry(offs[0:1, all_at], offs[1:2, all_at], offs[2:3, all_at])
        y_s[...] = jnp.concatenate(ys, axis=0)
        pre1, pre2 = radial_forward(w_in[0], w_mid[0], basis)
        pre1_out[:, all_at] = pre1
        pre2_out[:, all_at] = pre2
        w_edges[:, all_at] = dot_rows(out_stack, split_stack(silu(pre2)))

        def channels(c, carry):
            row = pl.multiple_of(c * CB, CB)
            acc = [jnp.zeros((CB, L), f32)] * 9
            for s in range(slots):
                at = pl.ds(pl.multiple_of(b * (L * slots) + s * L, L), L)
                f = f_out[pl.ds(row, CB), at]
                w = [w_edges[pl.ds(row + p * L, CB), at] * f for p in range(3)]
                acc[0] = acc[0] + w[0]
                for k in range(8):
                    y = y_s[k : k + 1, s * L : (s + 1) * L]
                    acc[1 + k] = acc[1 + k] + (w[1] if k < 3 else w[2]) * y
            for k in range(9):
                pooled[pl.ds(row + k * L, CB), pl.ds(pl.multiple_of(b * L, L), L)] = acc[k] / slots
            return carry

        lax.fori_loop(0, L // CB, channels, 0)
        here = pl.ds(pl.multiple_of(b * L, L), L)
        parts = [pooled[k * L : (k + 1) * L, here] for k in range(9)]
        new = node_one(parts, mats, outs, cs)
        kind = jnp.maximum(own[3:4], 0.0).astype(jnp.int32)
        hot = one_hot_columns(elements, kind)
        new[0] = new[0] + dot_rows(emb_stack, jnp.concatenate([hot, hot], axis=0))
        for k in range(9):
            rounded[k * L : (k + 1) * L, here] = new[k].astype(bf16)
        return carry

    lax.fori_loop(0, atoms // L, block, 0)
    border_feats[...] = dot(rounded[...], one_hot_columns(atoms, border[...])).astype(bf16)


def arrivals_kernel(
    grid, positions, kinds, keys, listed, counts, border, neighbours,
    nodes, idx, border_col, packet, arrived, sends, recvs,
):
    own_count = positions.shape[1]
    slot_count = listed.shape[1] // 4
    greet(grid)
    own = jnp.concatenate(
        [positions[...], kinds[...].astype(f32), jnp.zeros((4, own_count), f32)], axis=0
    )
    lane = lax.broadcasted_iota(jnp.int32, (8, L), 1)
    row = lax.broadcasted_iota(jnp.int32, (8, L), 0)
    used = jnp.zeros((8, L), jnp.int32)
    for d in range(4):
        used = jnp.where(lane // slot_count == d, counts[:, d : d + 1], used)
    leaving = exact_pick(own, one_hot_columns(own_count, listed[...]))
    leaving = jnp.where((row == 3) & (lane % slot_count >= used), -1.0, leaving)
    packet[:, 0:L] = exact_pick(own, one_hot_columns(own_count, border[...]))
    packet[:, L : 2 * L] = leaving
    copies = send_around(grid, -1, lambda q: packet, arrived, sends, recvs)
    own_row = lax.broadcasted_iota(jnp.int32, (8, own_count), 0)
    staying = jnp.where(keys[...] == 0, 1.0, 0.0)
    nodes[:, 0:own_count] = jnp.where(own_row == 4, staying, own)
    border_col[...] = column_of(border[...].astype(f32)).astype(jnp.int32)
    atoms, slots = neighbours.shape
    for b in range(atoms // L):
        block = neighbours[b * L : (b + 1) * L, :]
        block = jnp.where(block >= atoms + 5 * L, block - L, block).astype(f32)
        for s in range(slots):
            at = (b * slots + s) * L
            idx[:, at : at + L] = row_of(block[:, s : s + 1]).astype(jnp.int32)
    for copy in copies:
        copy.wait()
    incoming = jnp.zeros((8, L), f32)
    for d, (da, db) in enumerate([(-1, 0), (1, 0), (0, -1), (0, 1)]):
        shift = jnp.where(row == 0, float(da), 0.0) + jnp.where(row == 1, float(db), 0.0)
        piece = arrived[AROUND.index((da, db)), :, L : 2 * L] + shift
        incoming = jnp.where(lane // slot_count == d, piece, incoming)
    there = jnp.where(incoming[3:4] >= 0.0, 1.0, 0.0)
    nodes[:, own_count : own_count + L] = jnp.where(row == 4, there, incoming)
    first = own_count + L
    for q, (da, db) in enumerate(AROUND):
        shift = jnp.where(row == 0, float(da), 0.0) + jnp.where(row == 1, float(db), 0.0)
        shift = shift + jnp.where(row == 4, 1.0, 0.0)
        nodes[:, first + q * L : first + (q + 1) * L] = arrived[q, :, 0:L] + shift
    nodes[:, first + 8 * L : first + 9 * L] = jnp.zeros((8, L), f32)


def features_kernel(
    grid, feats, offs, idx, w_in, w_mid,
    h_out, pre1_out, pre2_out, y_out, ghosts, idx_col, sends, recvs,
):
    greet(grid)
    copies = send_around(grid, -1, lambda q: feats, ghosts, sends, recvs)
    edges = offs.shape[1] // 3

    def block(b, carry):
        at = pl.ds(pl.multiple_of(b * edges, L), edges)
        basis, ys = geometry(offs[0:1, at], offs[1:2, at], offs[2:3, at])
        y_out[:, at] = jnp.concatenate(ys, axis=0)
        pre1, pre2 = radial_forward(w_in[1], w_mid[1], basis)
        pre1_out[:, at] = pre1
        pre2_out[:, at] = pre2
        h_out[:, at] = split_stack(silu(pre2))
        return carry

    lax.fori_loop(0, 3, block, 0)

    def turn(t, carry):
        at = pl.ds(pl.multiple_of(t * L, L), L)
        idx_col[at, :] = column_of(idx[:, at].astype(f32)).astype(jnp.int32)
        return carry

    lax.fori_loop(0, offs.shape[1] // L, turn, 0)
    for copy in copies:
        copy.wait()


def features_back_kernel(
    grid, dghosts, dw, dy, pre1, pre2, offs, w_in, w_mid, w_out, doffs, back, sends, recvs
):
    greet(grid)
    copies = send_around(grid, 1, lambda q: dghosts.at[q], back, sends, recvs)
    blocks, _, edges = dw.shape

    def block(b, carry):
        at = pl.ds(pl.multiple_of(b * edges, L), edges)
        dbasis = radial_backward(
            w_out[...], w_mid[1], w_in[1], dw[b], pre1[:, at], pre2[:, at]
        )
        dys = tuple(
            jnp.sum(dy[k * 8 : (k + 1) * 8, at], axis=0, keepdims=True) for k in range(8)
        )
        _, pull = jax.vjp(geometry, offs[0:1, at], offs[1:2, at], offs[2:3, at])
        dx, dyy, dz = pull((dbasis, dys))
        doffs[:, at] = jnp.concatenate([dx, dyy, dz, jnp.zeros((5, edges), f32)], axis=0)
        return carry

    lax.fori_loop(0, blocks, block, 0)
    for copy in copies:
        copy.wait()


def forces_kernel(grid, dpos, border_col, forces, back, sends, recvs):
    atoms = forces.shape[1]
    greet(grid)
    copies = send_around(
        grid, 1, lambda q: dpos.at[:, atoms + q * L : atoms + (q + 1) * L], back, sends, recvs
    )
    hot = one_hot_rows(border_col[...], 0, atoms)
    for copy in copies:
        copy.wait()
    total = back[0]
    for q in range(1, 8):
        total = total + back[q]
    forces[...] = -(dpos[:, 0:atoms] + exact_pick(total, hot))[0:3]


def layer_two_kernel(
    rounded, ghosts, idx, idx_col, h_in, y_in, nodes,
    w_out, mix, out_mix, coefs, lin_in, hid_in, read_in,
    energy, dlocal, dghosts, dy_out, dw_out,
    table, dtable, dres, src, w_s, dw_s, pooled, dpooled, dw_sem,
):
    atoms = energy.shape[1]
    total = table.shape[1]
    slots = idx.shape[1] // atoms
    edges = slots * L
    occ = nodes[4:5, 0:atoms]
    out_stack = rows_stack(w_out[...])
    mats = [both_ways(mix[1, k]) for k in range(3)]
    out = both_ways(out_mix[...])
    hid = (rows_stack(hid_in[...]), hid_in[...])
    cs = [column_of(coefs[k : k + 1, :]) for k in range(3)]
    lin = column_of(lin_in[...])
    read = column_of(read_in[...])
    dtable[...] = jnp.zeros_like(dtable)
    table[:, 0:atoms] = rounded[...]
    for q in range(8):
        table[:, atoms + q * L : atoms + (q + 1) * L] = ghosts[q]
    table[:, atoms + 8 * L :] = jnp.zeros((table.shape[0], total - atoms - 8 * L), bf16)

    def block(b, carry):
        def gather(c, carry):
            at = pl.ds(pl.multiple_of(b * edges + c * G, G), G)
            to = pl.ds(pl.multiple_of(c * G, G), G)
            src[:, to] = dot(table[...], one_hot_columns(total, idx[:, at])).astype(bf16)
            w_s[:, to] = dot_rows(out_stack, h_in[:, at])
            return carry

        lax.fori_loop(0, edges // G, gather, 0)

        def load(row, s):
            at = slice(s * L, (s + 1) * L)
            f = [src[pl.ds(row + k * L, CB), at].astype(f32) for k in range(9)]
            w = [w_s[pl.ds(row + p * L, CB), at] for p in range(7)]
            far = pl.ds(pl.multiple_of(b * edges + s * L, L), L)
            y = [y_in[k : k + 1, far] for k in range(8)]
            return f, w, y

        def forward(c, carry):
            row = pl.multiple_of(c * CB, CB)
            acc = [jnp.zeros((CB, L), f32)] * 9
            for s in range(slots):
                f, w, y = load(row, s)
                along1 = f[1] * y[0] + f[2] * y[1] + f[3] * y[2]
                along2 = f[4] * y[3] + f[5] * y[4] + f[6] * y[5] + f[7] * y[6] + f[8] * y[7]
                acc[0] = acc[0] + w[0] * f[0] + w[1] * along1 + w[2] * along2
                s1, s2 = w[3] * f[0], w[5] * f[0]
                for k in range(3):
                    acc[1 + k] = acc[1 + k] + s1 * y[k] + w[4] * f[1 + k]
                for k in range(3, 8):
                    acc[1 + k] = acc[1 + k] + s2 * y[k] + w[6] * f[1 + k]
            for k in range(9):
                pooled[pl.ds(row + k * L, CB), :] = acc[k] / slots
            return carry

        lax.fori_loop(0, L // CB, forward, 0)
        here = pl.ds(pl.multiple_of(b * L, L), L)
        occupied = nodes[4:5, here]

        def node(parts, residual):
            return node_two(parts, residual, mats, out, cs, hid, read)

        residual = table[0:L, here].astype(f32)
        value, pull = jax.vjp(
            node, [pooled[k * L : (k + 1) * L, :] for k in range(9)], residual
        )
        linear = jnp.sum(lin * residual, axis=0, keepdims=True)
        energy[:, here] = (value + linear) * occupied
        dparts, dresidual = pull(occupied)
        for k in range(9):
            dpooled[k * L : (k + 1) * L, :] = dparts[k] / slots
        mine = pl.ds(pl.multiple_of(b * edges, L), edges)
        dy_out[:, mine] = jnp.zeros((64, edges), f32)

        def backward(c, carry):
            row = pl.multiple_of(c * CB, CB)
            g = [dpooled[pl.ds(row + k * L, CB), :] for k in range(9)]
            for s in range(slots):
                at = slice(s * L, (s + 1) * L)
                far = pl.ds(pl.multiple_of(b * edges + s * L, L), L)
                f, w, y = load(row, s)
                dw = [None] * 7
                dw[0] = g[0] * f[0]
                dw[1] = g[0] * (f[1] * y[0] + f[2] * y[1] + f[3] * y[2])
                dw[2] = g[0] * (
                    f[4] * y[3] + f[5] * y[4] + f[6] * y[5] + f[7] * y[6] + f[8] * y[7]
                )
                g1 = g[1] * y[0] + g[2] * y[1] + g[3] * y[2]
                g2 = g[4] * y[3] + g[5] * y[4] + g[6] * y[5] + g[7] * y[6] + g[8] * y[7]
                dw[3] = f[0] * g1
                dw[4] = g[1] * f[1] + g[2] * f[2] + g[3] * f[3]
                dw[5] = f[0] * g2
                dw[6] = g[4] * f[4] + g[5] * f[5] + g[6] * f[6] + g[7] * f[7] + g[8] * f[8]
                for p in range(7):
                    dw_s[pl.ds(row + p * L, CB), at] = dw[p].astype(bf16)
                v0, q0 = w[1] * g[0], w[2] * g[0]
                sv, sq = w[3] * f[0], w[5] * f[0]
                df = w[0] * g[0] + w[3] * g1 + w[5] * g2
                src[pl.ds(row, CB), at] = df.astype(bf16)
                for k in range(8):
                    base = v0 if k < 3 else q0
                    side = sv if k < 3 else sq
                    direct = w[4] if k < 3 else w[6]
                    dy = base * f[1 + k] + side * g[1 + k]
                    dy_out[k * 8 : (k + 1) * 8, far] += dy[0:8] + dy[8:16]
                    df = base * y[k] + direct * g[1 + k]
                    src[pl.ds(row + (1 + k) * L, CB), at] = df.astype(bf16)
            return carry

        lax.fori_loop(0, L // CB, backward, 0)

        keep = pltpu.make_async_copy(dw_s, dw_out.at[b], dw_sem)
        keep.start()

        def scatter(t, carry):
            to = pl.ds(pl.multiple_of(t * G, G), G)
            column = idx_col[pl.ds(pl.multiple_of(b * edges, 8), edges), :]
            part = dot(src[...], one_hot_rows(column, t * G, G))

            dtable[:, to] += part
            return carry

        lax.fori_loop(0, total // G, scatter, 0)
        keep.wait()
        dres[:, here] = dresidual
        return carry

    lax.fori_loop(0, atoms // L, block, 0)
    dlocal[...] = dtable[:, 0:atoms]
    dlocal[0:L, :] += dres[...] + lin * occ
    for q in range(8):
        dghosts[q] = dtable[:, atoms + q * L : atoms + (q + 1) * L].astype(bf16)


def layer_one_back_kernel(
    dlocal, back_in, border_col, idx_col, offs, doffs_two, f_in, w_in_edges, pre1_in, pre2_in, pooled,
    w_in, w_mid, w_out, mix, out_mix, coefs,
    dpos, dw_s, y_s, dy_s, dh_s, dpooled, d_s,
):
    atoms = dlocal.shape[1]
    total = dpos.shape[1]
    slots = offs.shape[1] // atoms
    edges = slots * L
    mats = [both_ways(mix[0, k]) for k in range(3)]
    outs = [both_ways(out_mix[k]) for k in range(3)]
    cs = [column_of(coefs[k : k + 1, :]) for k in range(5)]
    hot = one_hot_rows(border_col[...], 0, atoms)
    back = back_in[0].astype(f32)
    for q in range(1, 8):
        back = back + back_in[q].astype(f32)
    back_hi, back_lo = hi_lo(back)
    dh_s[...] = dlocal[...] + dot(back_hi, hot) + dot(back_lo, hot)
    dpos[...] = jnp.zeros_like(dpos)

    def block(b, carry):
        here = pl.ds(pl.multiple_of(b * L, L), L)
        _, pull = jax.vjp(
            lambda parts: node_one(parts, mats, outs, cs),
            [pooled[k * L : (k + 1) * L, here] for k in range(9)],
        )
        (dparts,) = pull([dh_s[k * L : (k + 1) * L, here] for k in range(9)])
        for k in range(9):
            dpooled[k * L : (k + 1) * L, :] = dparts[k] / slots

        mine = pl.ds(pl.multiple_of(b * edges, L), edges)
        _, ys = geometry(offs[0:1, mine], offs[1:2, mine], offs[2:3, mine])
        y_s[...] = jnp.concatenate(ys, axis=0)
        dy_s[...] = jnp.zeros_like(dy_s)

        def backward(c, carry):
            row = pl.multiple_of(c * CB, CB)
            g = [dpooled[pl.ds(row + k * L, CB), :] for k in range(9)]
            for s in range(slots):
                at = slice(s * L, (s + 1) * L)
                far = pl.ds(pl.multiple_of(b * edges + s * L, L), L)
                f = f_in[pl.ds(row, CB), far]
                y = [y_s[k : k + 1, at] for k in range(8)]
                dw_s[pl.ds(row, CB), at] = (g[0] * f).astype(bf16)
                g1 = g[1] * y[0] + g[2] * y[1] + g[3] * y[2]
                g2 = g[4] * y[3] + g[5] * y[4] + g[6] * y[5] + g[7] * y[6] + g[8] * y[7]
                dw_s[pl.ds(row + L, CB), at] = (f * g1).astype(bf16)
                dw_s[pl.ds(row + 2 * L, CB), at] = (f * g2).astype(bf16)
                w1 = w_in_edges[pl.ds(row + L, CB), far] * f
                w2 = w_in_edges[pl.ds(row + 2 * L, CB), far] * f
                for k in range(8):
                    dy = (w1 if k < 3 else w2) * g[1 + k]
                    dy_s[k * 8 : (k + 1) * 8, at] += dy[0:8] + dy[8:16]
            return carry

        lax.fori_loop(0, L // CB, backward, 0)

        dbasis = radial_backward(
            w_out[...], w_mid[0], w_in[0], dw_s[...], pre1_in[:, mine], pre2_in[:, mine]
        )
        dys = tuple(
            jnp.sum(dy_s[k * 8 : (k + 1) * 8, :], axis=0, keepdims=True) for k in range(8)
        )
        _, pull_again = jax.vjp(geometry, offs[0:1, mine], offs[1:2, mine], offs[2:3, mine])
        dx, dy, dz = pull_again((dbasis, dys))
        d = jnp.concatenate([dx, dy, dz, jnp.zeros((5, edges), f32)], axis=0) + doffs_two[:, mine]
        hi = d.astype(bf16).astype(f32)
        d_s[...] = jnp.concatenate([hi, d - hi], axis=0).astype(bf16)
        own = d[:, 0:L]
        for s in range(1, slots):
            own = own + d[:, s * L : (s + 1) * L]

        def scatter(t, carry):
            to = pl.ds(pl.multiple_of(t * G, G), G)
            column = idx_col[pl.ds(pl.multiple_of(b * edges, 8), edges), :]
            part = dot(d_s[...], one_hot_rows(column, t * G, G))
            dpos[:, to] += part[0:8] + part[8:16]
            return carry

        lax.fori_loop(0, total // G, scatter, 0)
        dpos[:, here] -= own
        return carry

    lax.fori_loop(0, atoms // L, block, 0)


def call(kernel, outs, scratch, *args, any_outs=(), remote=None):
    specs = [
        pl.BlockSpec(memory_space=pl.ANY if i in any_outs else pltpu.VMEM)
        for i in range(len(outs))
    ]
    semaphores = [pltpu.SemaphoreType.DMA(())] * len(any_outs)
    options = {}
    if remote is not None:
        semaphores = [pltpu.SemaphoreType.DMA((8,))] * 2
        options = dict(collective_id=remote, has_side_effects=True)
    return pl.pallas_call(
        kernel,
        out_shape=[jax.ShapeDtypeStruct(s, d) for s, d in outs],
        out_specs=specs,
        scratch_shapes=[pltpu.VMEM(s, d) for s, d in scratch] + semaphores,
        compiler_params=pltpu.CompilerParams(vmem_limit_bytes=VMEM_LIMIT, **options),
    )(*args)


def on_device(
    positions, species, dest_key, send_list, send_count, border, neighbours, embedding, radial_in,
    radial_mid, radial_out_one, radial_out_two, mix, mix_out_one, mix_out_two, product_one,
    product_two, read_lin, read_hidden, read_out,
):
    grid = (lax.axis_size("gx"), lax.axis_size("gy"))
    listed = send_list[0, 0]
    border_rows = border[0, 0]
    atoms, slots = neighbours.shape[2:]
    count = border_rows.shape[0]
    edge_total = atoms * slots
    total = atoms + 9 * count
    channels = embedding.shape[1]
    feats = 9 * channels

    edges = slots * L
    nodes, idx, border_col = call(
        functools.partial(arrivals_kernel, grid),
        [((8, total), f32), ((1, edge_total), jnp.int32), ((count, 1), jnp.int32)],
        [((8, 2 * L), f32), ((8, 8, 2 * L), f32)],
        positions[0, 0], species[0], dest_key[0], listed.reshape(1, -1), send_count[0],
        border_rows[None], neighbours[0, 0], remote=0,
    )
    hidden = radial_in.shape[2]
    rounded, border_feats, idx, offs, f_e, w_e, pre1, pre2, pooled = call(
        layer_one_kernel,
        [
            ((feats, atoms), bf16), ((feats, count), bf16), ((1, edge_total), jnp.int32),
            ((8, edge_total), f32), ((channels, edge_total), f32), ((3 * channels, edge_total), f32),
            ((hidden, edge_total), f32), ((hidden, edge_total), f32), ((feats, atoms), f32),
        ],
        [((8, edges), f32), ((-(-embedding.shape[0] // 16) * 16, channels), f32)],
        nodes, idx, embedding, radial_in, radial_mid, radial_out_one, mix, mix_out_one,
        product_one, border_rows[None],
    )
    h_two, pre1_two, pre2_two, y_two, ghosts, idx_col = call(
        functools.partial(features_kernel, grid),
        [
            ((3 * hidden, edge_total), bf16), ((hidden, edge_total), f32),
            ((hidden, edge_total), f32), ((8, edge_total), f32), ((8, feats, count), bf16),
            ((edge_total, 1), jnp.int32),
        ],
        [],
        border_feats, offs, idx, radial_in, radial_mid, remote=1,
    )
    energy, dlocal, dghosts, dy_two, dw_two = call(
        layer_two_kernel,
        [
            ((1, atoms), f32), ((feats, atoms), f32), ((8, feats, count), bf16),
            ((64, edge_total), f32), ((atoms // L, 7 * channels, edges), bf16),
        ],
        [
            ((feats, total), bf16), ((feats, total), f32), ((channels, atoms), f32),
            ((feats, edges), bf16), ((7 * channels, edges), f32),
            ((7 * channels, edges), bf16), ((feats, L), f32), ((feats, L), f32),
        ],
        rounded, ghosts, idx, idx_col, h_two, y_two, nodes, radial_out_two, mix, mix_out_two,
        product_two, read_lin[None], read_hidden, read_out[None], any_outs=(4,),
    )
    doffs, back = call(
        functools.partial(features_back_kernel, grid),
        [((8, edge_total), f32), ((8, feats, count), bf16)], [],
        dghosts, dw_two, dy_two, pre1_two, pre2_two, offs, radial_in, radial_mid,
        radial_out_two, remote=2,
    )
    (dpos,) = call(
        layer_one_back_kernel,
        [((8, total), f32)],
        [
            ((3 * channels, edges), bf16), ((8, edges), f32), ((64, edges), f32),
            ((feats, atoms), f32), ((feats, L), f32), ((16, edges), bf16),
        ],
        dlocal, back, border_col, idx_col, offs, doffs, f_e, w_e, pre1, pre2, pooled,
        radial_in, radial_mid, radial_out_one, mix, mix_out_one, product_one,
    )
    (forces,) = call(
        functools.partial(forces_kernel, grid),
        [((3, atoms), f32)], [((8, 8, L), f32)], dpos, border_col, remote=3,
    )
    return (energy[None], forces[None, None])


def solution(mesh):
    whole = P()
    in_specs = (
        P("gx", "gy", None, None),
        P("gx", "gy", None),
        P("gx", "gy", None),
        P("gx", "gy", None, None),
        P("gx", "gy", None),
        P("gx", "gy", None),
        P("gx", "gy", None, None),
    ) + (whole,) * 13
    out_specs = (P("gx", "gy", None), P("gx", "gy", None, None))
    return jax.shard_map(
        on_device, mesh=mesh, in_specs=in_specs, out_specs=out_specs, check_vma=False
    )
```

```python
import functools
import math

import jax
import jax.numpy as jnp
from jax import lax
from jax.experimental import pallas as pl
from jax.experimental.pallas import tpu as pltpu
from jax.sharding import PartitionSpec as P

f32 = jnp.float32
bf16 = jnp.bfloat16
CUT = 5.0
L = 128
G = 256
CB = 16
VMEM_LIMIT = 56 * 1024 * 1024


MESH = pl.DeviceIdType.MESH
AROUND = [(a - 1, b - 1) for a in range(3) for b in range(3) if (a, b) != (1, 1)]
CORNERS = [(-1, -1), (-1, 1), (1, -1), (1, 1)]
ORDER = sorted(range(8), key=lambda q: -abs(AROUND[q][1]))


def cell(grid, da, db):
    x, y = lax.axis_index("gx"), lax.axis_index("gy")
    return (lax.rem(x + da + grid[0], grid[0]), lax.rem(y + db + grid[1], grid[1]))


def greet(grid):
    barrier = pltpu.get_barrier_semaphore()
    for da, db in AROUND:
        pl.semaphore_signal(barrier, inc=1, device_id=cell(grid, da, db), device_id_type=MESH)
    pl.semaphore_wait(barrier, 8)


def greet_sides(grid):
    barrier = pltpu.get_barrier_semaphore()
    for da, db in ((1, 0), (-1, 0), (0, 1), (0, -1)):
        pl.semaphore_signal(barrier, inc=1, device_id=cell(grid, da, db), device_id_type=MESH)
    pl.semaphore_wait(barrier, 4)


def at_cell(da, db):
    return AROUND.index((da, db))


def half_of(array, h):
    rows = array.shape[0] // 2
    return array.at[pl.ds(h * rows, rows), :]


def send_half(grid, place, h, source, target, to, sends, recvs):
    copy = pltpu.make_async_remote_copy(
        src_ref=source,
        dst_ref=target,
        send_sem=sends.at[place, h],
        recv_sem=recvs.at[place, h],
        device_id=cell(grid, *to),
        device_id_type=MESH,
    )
    copy.start()
    return copy


def send_around(grid, sign, source, target, sends, recvs):
    copies = []
    for q in ORDER:
        da, db = AROUND[q]
        copy = pltpu.make_async_remote_copy(
            src_ref=source(q),
            dst_ref=target.at[q],
            send_sem=sends.at[q],
            recv_sem=recvs.at[q],
            device_id=cell(grid, sign * da, sign * db),
            device_id_type=MESH,
        )
        copy.start()
        copies.append(copy)
    return copies


def three_parts(x):
    hi = x.astype(bf16).astype(f32)
    mid = (x - hi).astype(bf16).astype(f32)
    return jnp.concatenate([hi, mid, x - hi - mid, jnp.zeros_like(x)], axis=0).astype(bf16)


def exact_pick(x, hot):
    got = dot(three_parts(x), hot)
    return got[0:8] + got[8:16] + got[16:24]


def dot(a, b):
    return jnp.dot(a, b, preferred_element_type=f32)


def hi_lo(x):
    hi = x.astype(bf16)
    return hi, (x - hi.astype(f32)).astype(bf16)


def split_stack(x):
    hi, lo = hi_lo(x)
    return jnp.concatenate([hi, hi, lo], axis=0)


def split_stack_small(x):
    hi = x.astype(bf16).astype(f32)
    return jnp.concatenate([hi, hi, x - hi], axis=0).astype(bf16)


def rows_stack(w):
    if w.shape[0] % 16:
        hi = w.astype(bf16).astype(f32)
        return jnp.concatenate([hi, w - hi, hi], axis=0).astype(bf16)
    hi, lo = hi_lo(w)
    return jnp.concatenate([hi, lo, hi], axis=0)


def lanes_stack(w):
    hi, lo = hi_lo(w)
    return jnp.concatenate([hi, lo, hi], axis=1)


def dot_rows(stack, x_stack):
    return lax.dot_general(
        stack, x_stack, (((0,), (0,)), ((), ())), preferred_element_type=f32
    )


def dot_back(w, x):
    w_hi, w_lo = hi_lo(w)
    x_hi, x_lo = hi_lo(x)
    return dot(w_hi, x_hi) + dot(w_lo, x_hi) + dot(w_hi, x_lo)


def column_of(row):
    size = row.shape[1]
    down = lax.broadcasted_iota(jnp.int32, (size, size), 0)
    along = lax.broadcasted_iota(jnp.int32, (size, size), 1)
    return jnp.sum(jnp.where(down == along, row, 0.0), axis=1, keepdims=True)


def silu(x):
    return x * jax.nn.sigmoid(x)


def silu_slope(x):
    sig = jax.nn.sigmoid(x)
    return sig * (1.0 + x * (1.0 - sig))


def geometry(ox, oy, oz):
    squared = ox * ox + oy * oy + oz * oz + 1.0
    distance = jnp.sqrt(squared)
    inverse = 1.0 / distance
    ux, uy, uz = ox * inverse, oy * inverse, oz * inverse
    t = distance / CUT
    sixth = t * t * t * t * t * t
    envelope = 1.0 - 28.0 * sixth + 48.0 * sixth * t - 21.0 * sixth * t * t
    orders = (lax.broadcasted_iota(jnp.int32, (8, ox.shape[1]), 0) + 1).astype(f32)
    wave = jnp.sin(orders * (math.pi / CUT) * jnp.broadcast_to(distance, orders.shape))
    scale = math.sqrt(2.0 / CUT) * envelope * inverse
    basis = wave * jnp.broadcast_to(scale, orders.shape)
    r3, r5, r15 = math.sqrt(3.0), math.sqrt(5.0), math.sqrt(15.0)
    harmonics = (
        r3 * ux,
        r3 * uy,
        r3 * uz,
        r15 * ux * uy,
        r15 * uy * uz,
        0.5 * r5 * (2.0 * uz * uz - ux * ux - uy * uy),
        r15 * ux * uz,
        0.5 * r15 * (ux * ux - uy * uy),
    )
    return basis, harmonics


def one_hot_columns(rows, index_row):
    place = lax.broadcasted_iota(jnp.int32, (rows, index_row.shape[1]), 0)
    return jnp.where(place == index_row, 1.0, 0.0).astype(bf16)


def one_hot_rows(index_column, base, columns):
    place = lax.broadcasted_iota(jnp.int32, (index_column.shape[0], columns), 1) + base
    return jnp.where(place == index_column, 1.0, 0.0).astype(bf16)


@jax.custom_vjp
def mixed(w, x):
    return dot_rows(w[0], split_stack(x))


def mixed_fwd(w, x):
    return mixed(w, x), w


def mixed_bwd(w, g):
    return None, dot(w[1], split_stack(g))


mixed.defvjp(mixed_fwd, mixed_bwd)


@jax.custom_vjp
def mixed_across(w, x):
    return dot(w[0], split_stack(x))


def mixed_across_fwd(w, x):
    return mixed_across(w, x), w


def mixed_across_bwd(w, g):
    return None, dot_rows(w[1], split_stack(g))


mixed_across.defvjp(mixed_across_fwd, mixed_across_bwd)


def both_ways(w):
    return rows_stack(w), lanes_stack(w)


def mix_orders(mats, parts):
    scalar = mixed(mats[0], parts[0])
    vector = mixed(mats[1], jnp.concatenate(parts[1:4], axis=1))
    tensor = mixed(mats[2], jnp.concatenate(parts[4:9], axis=1))
    return scalar, [vector[:, i * L : (i + 1) * L] for i in range(3)], [
        tensor[:, i * L : (i + 1) * L] for i in range(5)
    ]


def product_scalar(coefs, s, v, q):
    total = s + coefs[0] * s * s
    total = total + coefs[1] * (v[0] * v[0] + v[1] * v[1] + v[2] * v[2])
    return total + coefs[2] * (
        q[0] * q[0] + q[1] * q[1] + q[2] * q[2] + q[3] * q[3] + q[4] * q[4]
    )


def node_one(parts, mats, outs, coefs):
    s, v, q = mix_orders(mats, parts)
    b0 = product_scalar(coefs, s, v, q)
    gate1 = 1.0 + coefs[3] * s
    gate2 = 1.0 + coefs[4] * s
    s, v, q = mix_orders(outs, [b0] + [x * gate1 for x in v] + [x * gate2 for x in q])
    return [s] + v + q


def node_two(parts, residual, mats, out, coefs, hid, read):
    s, v, q = mix_orders(mats, parts)
    scalars = mixed(out, product_scalar(coefs, s, v, q)) + residual
    hidden = silu(mixed_across(hid, scalars))
    return jnp.sum(read * hidden, axis=0, keepdims=True)


def radial_forward(w_in, w_mid, basis):
    pre1 = dot_rows(rows_stack(w_in), split_stack_small(basis))
    pre2 = dot_rows(rows_stack(w_mid), split_stack(silu(pre1)))
    return pre1, pre2


def radial_backward(w_out, w_mid, w_in, dw, pre1, pre2):
    both = dot(jnp.concatenate(hi_lo(w_out), axis=0), dw)
    half = both.shape[0] // 2
    dpre2 = (both[:half] + both[half:]) * silu_slope(pre2)
    dpre1 = dot_back(w_mid, dpre2) * silu_slope(pre1)
    return dot_back(w_in, dpre1)


def layer_one_kernel(
    nodes, idx, emb, w_in, w_mid, w_out, mix, out_mix, coefs, border,
    rounded, border_feats, idx_out, offs, f_out, w_edges, pre1_out, pre2_out, pooled, y_s, emb_s,
):
    atoms = rounded.shape[1]
    total = nodes.shape[1]
    slots = idx.shape[1] // atoms
    stack = three_parts(nodes[...])
    elements = emb_s.shape[0]
    emb_s[...] = jnp.zeros_like(emb_s)
    emb_s[0 : emb.shape[0], :] = emb[...]
    emb_stack = jnp.concatenate(hi_lo(emb_s[...]), axis=0)
    out_stack = rows_stack(w_out[...])
    mats = [both_ways(mix[0, k]) for k in range(3)]
    outs = [both_ways(out_mix[k]) for k in range(3)]
    cs = [column_of(coefs[k : k + 1, :]) for k in range(5)]

    def block(b, carry):
        own = nodes[:, pl.ds(pl.multiple_of(b * L, L), L)]
        own2 = jnp.concatenate([own, own], axis=1)

        def gather(c, carry):
            at = pl.ds(pl.multiple_of(b * (L * slots) + c * G, G), G)
            index = idx[:, at]
            got = dot(stack, one_hot_columns(total, index))
            got = got[0:8] + got[8:16] + got[16:24]
            valid = (index >= 0) & (got[4:5] * own2[4:5] > 0.5)
            idx_out[:, at] = jnp.where(valid, index, -1)
            offset = got - own2
            offs[:, at] = offset
            kind = jnp.where(valid, jnp.maximum(got[3:4], 0.0).astype(jnp.int32), -1)
            hot = one_hot_columns(elements, kind)
            f_out[:, at] = dot_rows(emb_stack, jnp.concatenate([hot, hot], axis=0))
            return carry

        lax.fori_loop(0, slots * L // G, gather, 0, unroll=2)
        all_at = pl.ds(pl.multiple_of(b * (L * slots), L), L * slots)
        basis, ys = geometry(offs[0:1, all_at], offs[1:2, all_at], offs[2:3, all_at])
        y_s[...] = jnp.concatenate(ys, axis=0)
        pre1, pre2 = radial_forward(w_in[0], w_mid[0], basis)
        pre1_out[:, all_at] = pre1
        pre2_out[:, all_at] = pre2
        w_edges[:, all_at] = dot_rows(out_stack, split_stack(silu(pre2)))

        def channels(c, carry):
            row = pl.multiple_of(c * CB, CB)
            acc = [jnp.zeros((CB, L), f32)] * 9
            for s in range(slots):
                at = pl.ds(pl.multiple_of(b * (L * slots) + s * L, L), L)
                f = f_out[pl.ds(row, CB), at]
                w = [w_edges[pl.ds(row + p * L, CB), at] * f for p in range(3)]
                acc[0] = acc[0] + w[0]
                for k in range(8):
                    y = y_s[k : k + 1, s * L : (s + 1) * L]
                    acc[1 + k] = acc[1 + k] + (w[1] if k < 3 else w[2]) * y
            for k in range(9):
                pooled[pl.ds(row + k * L, CB), pl.ds(pl.multiple_of(b * L, L), L)] = acc[k] / slots
            return carry

        lax.fori_loop(0, L // CB, channels, 0)
        here = pl.ds(pl.multiple_of(b * L, L), L)
        parts = [pooled[k * L : (k + 1) * L, here] for k in range(9)]
        new = node_one(parts, mats, outs, cs)
        kind = jnp.maximum(own[3:4], 0.0).astype(jnp.int32)
        hot = one_hot_columns(elements, kind)
        new[0] = new[0] + dot_rows(emb_stack, jnp.concatenate([hot, hot], axis=0))
        for k in range(9):
            rounded[k * L : (k + 1) * L, here] = new[k].astype(bf16)
        return carry

    lax.fori_loop(0, atoms // L, block, 0)
    border_feats[...] = dot(rounded[...], one_hot_columns(atoms, border[...])).astype(bf16)


def arrivals_kernel(
    grid, positions, kinds, keys, listed, counts, border, neighbours,
    nodes, idx, border_col, packet, arrived, sends, recvs,
):
    own_count = positions.shape[2]
    slot_count = listed.shape[1] // 4
    greet(grid)
    own = jnp.concatenate(
        [positions[0], positions[1], positions[2], kinds[...].astype(f32)]
        + [jnp.zeros((4, own_count), f32)],
        axis=0,
    )
    lane = lax.broadcasted_iota(jnp.int32, (8, L), 1)
    row = lax.broadcasted_iota(jnp.int32, (8, L), 0)
    used = jnp.zeros((8, L), jnp.int32)
    for d in range(4):
        used = jnp.where(lane // slot_count == d, counts[:, d : d + 1], used)
    leaving = exact_pick(own, one_hot_columns(own_count, listed[...]))
    leaving = jnp.where((row == 3) & (lane % slot_count >= used), -1.0, leaving)
    packet[:, 0:L] = exact_pick(own, one_hot_columns(own_count, border[...]))
    packet[:, L : 2 * L] = leaving
    copies = send_around(grid, -1, lambda q: packet, arrived, sends, recvs)
    own_row = lax.broadcasted_iota(jnp.int32, (8, own_count), 0)
    staying = jnp.where(keys[...] == 0, 1.0, 0.0)
    nodes[:, 0:own_count] = jnp.where(own_row == 4, staying, own)
    border_col[...] = column_of(border[...].astype(f32)).astype(jnp.int32)
    slots, _, atoms = neighbours.shape
    for b in range(atoms // L):
        for s in range(slots):
            at = (b * slots + s) * L
            listing = neighbours[s, :, b * L : (b + 1) * L]
            idx[:, at : at + L] = jnp.where(listing >= atoms + 5 * L, listing - L, listing)
    for copy in copies:
        copy.wait()
    incoming = jnp.zeros((8, L), f32)
    for d, (da, db) in enumerate([(-1, 0), (1, 0), (0, -1), (0, 1)]):
        shift = jnp.where(row == 0, float(da), 0.0) + jnp.where(row == 1, float(db), 0.0)
        piece = arrived[AROUND.index((da, db)), :, L : 2 * L] + shift
        incoming = jnp.where(lane // slot_count == d, piece, incoming)
    there = jnp.where(incoming[3:4] >= 0.0, 1.0, 0.0)
    nodes[:, own_count : own_count + L] = jnp.where(row == 4, there, incoming)
    first = own_count + L
    for q, (da, db) in enumerate(AROUND):
        shift = jnp.where(row == 0, float(da), 0.0) + jnp.where(row == 1, float(db), 0.0)
        shift = shift + jnp.where(row == 4, 1.0, 0.0)
        nodes[:, first + q * L : first + (q + 1) * L] = arrived[q, :, 0:L] + shift
    nodes[:, first + 8 * L : first + 9 * L] = jnp.zeros((8, L), f32)


def features_kernel(
    grid, feats, offs, idx, w_in, w_mid,
    h_out, pre1_out, pre2_out, y_out, ghosts, idx_col, sends, recvs,
):
    greet_sides(grid)

    def send(h, da, db, source, to):
        place = at_cell(da, db)
        target = half_of(ghosts.at[place], h)
        return send_half(grid, place, h, source, target, to, sends, recvs)

    def send_across(h):
        mine = half_of(feats, h)
        return [send(h, -1, 0, mine, (1, 0)), send(h, 1, 0, mine, (-1, 0))]

    across = [send_across(0)]
    others = []
    for h in range(2):
        mine = half_of(feats, h)
        others.append(send(h, 0, -1, mine, (0, 1)))
        others.append(send(h, 0, 1, mine, (0, -1)))
    edges = offs.shape[1] // 3

    def block(b, carry):
        at = pl.ds(pl.multiple_of(b * edges, L), edges)
        basis, ys = geometry(offs[0:1, at], offs[1:2, at], offs[2:3, at])
        y_out[:, at] = jnp.concatenate(ys, axis=0)
        pre1, pre2 = radial_forward(w_in[1], w_mid[1], basis)
        pre1_out[:, at] = pre1
        pre2_out[:, at] = pre2
        h_out[:, at] = split_stack(silu(pre2))
        return carry

    lax.fori_loop(0, 3, block, 0)
    across.append(send_across(1))

    def turn(t, carry):
        at = pl.ds(pl.multiple_of(t * L, L), L)
        idx_col[at, :] = column_of(idx[:, at].astype(f32)).astype(jnp.int32)
        return carry

    lax.fori_loop(0, offs.shape[1] // L, turn, 0)
    for h in range(2):
        for da, copy in zip((-1, 1), across[h]):
            copy.wait()
            landed = half_of(ghosts.at[at_cell(da, 0)], h)
            others.append(send(h, da, -1, landed, (0, 1)))
            others.append(send(h, da, 1, landed, (0, -1)))
    for copy in others:
        copy.wait()


def features_back_kernel(
    grid, dghosts, dw, dy, pre1, pre2, offs, w_in, w_mid, w_out, doffs, back,
    dw_s, corner, total, sends, recvs, dw_sem,
):
    greet_sides(grid)
    blocks, _, edges = dw.shape

    def send_corners(h):
        copies = []
        for i, (da, db) in enumerate(CORNERS):
            place = at_cell(da, db)
            copies.append(
                send_half(
                    grid, place, h, half_of(dghosts.at[place], h), half_of(corner.at[i], h),
                    (0, db), sends, recvs,
                )
            )
        return copies

    def send_sums(h):
        copies = []
        rows = dghosts.shape[1] // 2
        at = slice(h * rows, (h + 1) * rows)
        for i, da in enumerate((-1, 1)):
            place = at_cell(da, 0)
            total[i, at, :] = (
                dghosts[place, at, :].astype(f32)
                + corner[2 * i, at, :].astype(f32)
                + corner[2 * i + 1, at, :].astype(f32)
            ).astype(bf16)
            copies.append(
                send_half(
                    grid, place, h, half_of(total.at[i], h), half_of(back.at[i], h),
                    (da, 0), sends, recvs,
                )
            )
        return copies

    def block(b):
        fetch = pltpu.make_async_copy(dw.at[b], dw_s, dw_sem)
        fetch.start()
        fetch.wait()
        at = slice(b * edges, (b + 1) * edges)
        dbasis = radial_backward(
            w_out[...], w_mid[1], w_in[1], dw_s[...], pre1[:, at], pre2[:, at]
        )
        dys = tuple(
            jnp.sum(dy[k * 8 : (k + 1) * 8, at], axis=0, keepdims=True) for k in range(8)
        )
        _, pull = jax.vjp(geometry, offs[0:1, at], offs[1:2, at], offs[2:3, at])
        dx, dyy, dz = pull((dbasis, dys))
        doffs[:, at] = jnp.concatenate([dx, dyy, dz, jnp.zeros((5, edges), f32)], axis=0)

    early = send_corners(0)
    block(0)
    late = send_corners(1)
    for b in range(1, blocks - 1):
        block(b)
    for copy in early:
        copy.wait()
    rest = send_sums(0)
    for i, db in enumerate((-1, 1)):
        place = at_cell(0, db)
        for h in range(2):
            rest.append(
                send_half(
                    grid, place, h, half_of(dghosts.at[place], h), half_of(back.at[2 + i], h),
                    (0, db), sends, recvs,
                )
            )
    block(blocks - 1)
    for copy in late:
        copy.wait()
    rest += send_sums(1)
    for copy in rest:
        copy.wait()


def forces_kernel(grid, dpos, border_col, forces, back, sends, recvs):
    atoms = forces.shape[1]
    greet(grid)
    copies = send_around(
        grid, 1, lambda q: dpos.at[:, atoms + q * L : atoms + (q + 1) * L], back, sends, recvs
    )
    hot = one_hot_rows(border_col[...], 0, atoms)
    for copy in copies:
        copy.wait()
    total = back[0]
    for q in range(1, 8):
        total = total + back[q]
    forces[...] = -(dpos[:, 0:atoms] + exact_pick(total, hot))[0:3]


def layer_two_kernel(
    rounded, ghosts, idx, idx_col, h_in, y_in, nodes,
    w_out, mix, out_mix, coefs, lin_in, hid_in, read_in,
    energy, dlocal, dghosts, dy_out, dw_out,
    table, dtable, dres, src, w_s, dw_s, pooled, dpooled, dw_sem,
):
    atoms = energy.shape[1]
    total = table.shape[1]
    slots = idx.shape[1] // atoms
    edges = slots * L
    occ = nodes[4:5, 0:atoms]
    out_stack = rows_stack(w_out[...])
    mats = [both_ways(mix[1, k]) for k in range(3)]
    out = both_ways(out_mix[...])
    hid = (lanes_stack(hid_in[...]), rows_stack(hid_in[...]))
    cs = [column_of(coefs[k : k + 1, :]) for k in range(3)]
    lin = column_of(lin_in[...])
    read = column_of(read_in[...])
    table[:, 0:atoms] = rounded[...]
    for q in range(8):
        table[:, atoms + q * L : atoms + (q + 1) * L] = ghosts[q]
    table[:, atoms + 8 * L :] = jnp.zeros((table.shape[0], total - atoms - 8 * L), bf16)

    def block(b, carry):
        def gather(c, carry):
            at = pl.ds(pl.multiple_of(b * edges + c * G, G), G)
            src[:, at] = dot(table[...], one_hot_columns(total, idx[:, at])).astype(bf16)
            return carry

        lax.fori_loop(0, edges // G, gather, 0, unroll=2)
        w_s[...] = dot_rows(out_stack, h_in[:, pl.ds(pl.multiple_of(b * edges, L), edges)])

        def load(row, s):
            at = slice(s * L, (s + 1) * L)
            far = pl.ds(pl.multiple_of(b * edges + s * L, L), L)
            f = [src[pl.ds(row + k * L, CB), far].astype(f32) for k in range(9)]
            w = [w_s[pl.ds(row + p * L, CB), at] for p in range(7)]
            y = [y_in[k : k + 1, far] for k in range(8)]
            return f, w, y

        def forward(c, carry):
            row = pl.multiple_of(c * CB, CB)
            acc = [jnp.zeros((CB, L), f32)] * 9
            for s in range(slots):
                f, w, y = load(row, s)
                along1 = f[1] * y[0] + f[2] * y[1] + f[3] * y[2]
                along2 = f[4] * y[3] + f[5] * y[4] + f[6] * y[5] + f[7] * y[6] + f[8] * y[7]
                acc[0] = acc[0] + w[0] * f[0] + w[1] * along1 + w[2] * along2
                s1, s2 = w[3] * f[0], w[5] * f[0]
                for k in range(3):
                    acc[1 + k] = acc[1 + k] + s1 * y[k] + w[4] * f[1 + k]
                for k in range(3, 8):
                    acc[1 + k] = acc[1 + k] + s2 * y[k] + w[6] * f[1 + k]
            for k in range(9):
                pooled[pl.ds(row + k * L, CB), :] = acc[k] / slots
            return carry

        lax.fori_loop(0, L // CB, forward, 0)
        here = pl.ds(pl.multiple_of(b * L, L), L)
        occupied = nodes[4:5, here]

        def node(parts, residual):
            return node_two(parts, residual, mats, out, cs, hid, read)

        residual = table[0:L, here].astype(f32)
        value, pull = jax.vjp(
            node, [pooled[k * L : (k + 1) * L, :] for k in range(9)], residual
        )
        linear = jnp.sum(lin * residual, axis=0, keepdims=True)
        energy[:, here] = (value + linear) * occupied
        dparts, dresidual = pull(occupied)
        for k in range(9):
            dpooled[k * L : (k + 1) * L, :] = dparts[k] / slots
        mine = pl.ds(pl.multiple_of(b * edges, L), edges)
        dy_out[:, mine] = jnp.zeros((64, edges), f32)

        def backward(c, carry):
            row = pl.multiple_of(c * CB, CB)
            g = [dpooled[pl.ds(row + k * L, CB), :] for k in range(9)]
            for s in range(slots):
                at = slice(s * L, (s + 1) * L)
                far = pl.ds(pl.multiple_of(b * edges + s * L, L), L)
                f, w, y = load(row, s)
                dw = [None] * 7
                dw[0] = g[0] * f[0]
                dw[1] = g[0] * (f[1] * y[0] + f[2] * y[1] + f[3] * y[2])
                dw[2] = g[0] * (
                    f[4] * y[3] + f[5] * y[4] + f[6] * y[5] + f[7] * y[6] + f[8] * y[7]
                )
                g1 = g[1] * y[0] + g[2] * y[1] + g[3] * y[2]
                g2 = g[4] * y[3] + g[5] * y[4] + g[6] * y[5] + g[7] * y[6] + g[8] * y[7]
                dw[3] = f[0] * g1
                dw[4] = g[1] * f[1] + g[2] * f[2] + g[3] * f[3]
                dw[5] = f[0] * g2
                dw[6] = g[4] * f[4] + g[5] * f[5] + g[6] * f[6] + g[7] * f[7] + g[8] * f[8]
                for p in range(7):
                    dw_s[b, pl.ds(row + p * L, CB), at] = dw[p].astype(bf16)
                v0, q0 = w[1] * g[0], w[2] * g[0]
                sv, sq = w[3] * f[0], w[5] * f[0]
                df = w[0] * g[0] + w[3] * g1 + w[5] * g2
                src[pl.ds(row, CB), far] = df.astype(bf16)
                for k in range(8):
                    base = v0 if k < 3 else q0
                    side = sv if k < 3 else sq
                    direct = w[4] if k < 3 else w[6]
                    dy = base * f[1 + k] + side * g[1 + k]
                    dy_out[k * 8 : (k + 1) * 8, far] += dy[0:8] + dy[8:16]
                    df = base * y[k] + direct * g[1 + k]
                    src[pl.ds(row + (1 + k) * L, CB), far] = df.astype(bf16)
            return carry

        lax.fori_loop(0, L // CB, backward, 0)

        pltpu.make_async_copy(dw_s.at[b], dw_out.at[b], dw_sem.at[b]).start()
        dres[:, here] = dresidual
        return carry

    lax.fori_loop(0, atoms // L, block, 0)

    def scatter(t, carry):
        to = pl.ds(pl.multiple_of(t * G, G), G)
        dtable[:, to] = dot(src[...], one_hot_rows(idx_col[...], t * G, G))
        return carry

    lax.fori_loop(0, total // G, scatter, 0)
    for b in range(atoms // L):
        pltpu.make_async_copy(dw_s.at[b], dw_out.at[b], dw_sem.at[b]).wait()
    dlocal[...] = dtable[:, 0:atoms]
    dlocal[0:L, :] += dres[...] + lin * occ
    for q in range(8):
        dghosts[q] = dtable[:, atoms + q * L : atoms + (q + 1) * L].astype(bf16)


def layer_one_back_kernel(
    dlocal, back_in, border_col, idx_col, offs, doffs_two, f_in, w_in_edges, pre1_in, pre2_in, pooled,
    w_in, w_mid, w_out, mix, out_mix, coefs,
    dpos, dw_s, y_s, dy_s, dh_s, dpooled, d_s,
):
    atoms = dlocal.shape[1]
    total = dpos.shape[1]
    slots = offs.shape[1] // atoms
    edges = slots * L
    mats = [both_ways(mix[0, k]) for k in range(3)]
    outs = [both_ways(out_mix[k]) for k in range(3)]
    cs = [column_of(coefs[k : k + 1, :]) for k in range(5)]
    hot = one_hot_rows(border_col[...], 0, atoms)
    back = back_in[0].astype(f32)
    for q in range(1, 4):
        back = back + back_in[q].astype(f32)
    back_hi, back_lo = hi_lo(back)
    dh_s[...] = dlocal[...] + dot(back_hi, hot) + dot(back_lo, hot)
    dpos[...] = jnp.zeros_like(dpos)

    def block(b, carry):
        here = pl.ds(pl.multiple_of(b * L, L), L)
        _, pull = jax.vjp(
            lambda parts: node_one(parts, mats, outs, cs),
            [pooled[k * L : (k + 1) * L, here] for k in range(9)],
        )
        (dparts,) = pull([dh_s[k * L : (k + 1) * L, here] for k in range(9)])
        for k in range(9):
            dpooled[k * L : (k + 1) * L, :] = dparts[k] / slots

        mine = pl.ds(pl.multiple_of(b * edges, L), edges)
        _, ys = geometry(offs[0:1, mine], offs[1:2, mine], offs[2:3, mine])
        y_s[...] = jnp.concatenate(ys, axis=0)
        dy_s[...] = jnp.zeros_like(dy_s)

        def backward(c, carry):
            row = pl.multiple_of(c * CB, CB)
            g = [dpooled[pl.ds(row + k * L, CB), :] for k in range(9)]
            for s in range(slots):
                at = slice(s * L, (s + 1) * L)
                far = pl.ds(pl.multiple_of(b * edges + s * L, L), L)
                f = f_in[pl.ds(row, CB), far]
                y = [y_s[k : k + 1, at] for k in range(8)]
                dw_s[pl.ds(row, CB), at] = (g[0] * f).astype(bf16)
                g1 = g[1] * y[0] + g[2] * y[1] + g[3] * y[2]
                g2 = g[4] * y[3] + g[5] * y[4] + g[6] * y[5] + g[7] * y[6] + g[8] * y[7]
                dw_s[pl.ds(row + L, CB), at] = (f * g1).astype(bf16)
                dw_s[pl.ds(row + 2 * L, CB), at] = (f * g2).astype(bf16)
                w1 = w_in_edges[pl.ds(row + L, CB), far] * f
                w2 = w_in_edges[pl.ds(row + 2 * L, CB), far] * f
                for k in range(8):
                    dy = (w1 if k < 3 else w2) * g[1 + k]
                    dy_s[k * 8 : (k + 1) * 8, at] += dy[0:8] + dy[8:16]
            return carry

        lax.fori_loop(0, L // CB, backward, 0)

        dbasis = radial_backward(
            w_out[...], w_mid[0], w_in[0], dw_s[...], pre1_in[:, mine], pre2_in[:, mine]
        )
        dys = tuple(
            jnp.sum(dy_s[k * 8 : (k + 1) * 8, :], axis=0, keepdims=True) for k in range(8)
        )
        _, pull_again = jax.vjp(geometry, offs[0:1, mine], offs[1:2, mine], offs[2:3, mine])
        dx, dy, dz = pull_again((dbasis, dys))
        d = jnp.concatenate([dx, dy, dz, jnp.zeros((5, edges), f32)], axis=0) + doffs_two[:, mine]
        hi = d.astype(bf16).astype(f32)
        d_s[...] = jnp.concatenate([hi, d - hi], axis=0).astype(bf16)
        own = d[:, 0:L]
        for s in range(1, slots):
            own = own + d[:, s * L : (s + 1) * L]

        def scatter(t, carry):
            to = pl.ds(pl.multiple_of(t * G, G), G)
            column = idx_col[pl.ds(pl.multiple_of(b * edges, 8), edges), :]
            part = dot(d_s[...], one_hot_rows(column, t * G, G))
            dpos[:, to] += part[0:8] + part[8:16]
            return carry

        lax.fori_loop(0, total // G, scatter, 0)
        dpos[:, here] -= own
        return carry

    lax.fori_loop(0, atoms // L, block, 0)


def call(kernel, outs, scratch, *args, any_ins=(), any_outs=(), semaphores=(), remote=None):
    def places(count, anywhere):
        return [
            pl.BlockSpec(memory_space=pl.ANY if i in anywhere else pltpu.VMEM) for i in range(count)
        ]

    semaphores = [pltpu.SemaphoreType.DMA(shape) for shape in semaphores]
    options = {}
    if remote is not None:
        options = dict(collective_id=remote, has_side_effects=True)
    return pl.pallas_call(
        kernel,
        out_shape=[jax.ShapeDtypeStruct(s, d) for s, d in outs],
        in_specs=places(len(args), any_ins),
        out_specs=places(len(outs), any_outs),
        scratch_shapes=[pltpu.VMEM(s, d) for s, d in scratch] + semaphores,
        compiler_params=pltpu.CompilerParams(vmem_limit_bytes=VMEM_LIMIT, **options),
    )(*args)


def on_device(
    positions, species, dest_key, send_list, send_count, border, neighbours, embedding, radial_in,
    radial_mid, radial_out_one, radial_out_two, mix, mix_out_one, mix_out_two, product_one,
    product_two, read_lin, read_hidden, read_out,
):
    grid = (lax.axis_size("gx"), lax.axis_size("gy"))
    listed = send_list[0, 0]
    border_rows = border[0, 0]
    atoms, slots = neighbours.shape[2:]
    count = border_rows.shape[0]
    edge_total = atoms * slots
    total = atoms + 9 * count
    channels = embedding.shape[1]
    feats = 9 * channels

    edges = slots * L
    nodes, idx, border_col = call(
        functools.partial(arrivals_kernel, grid),
        [((8, total), f32), ((1, edge_total), jnp.int32), ((count, 1), jnp.int32)],
        [((8, 2 * L), f32), ((8, 8, 2 * L), f32)],
        positions[0].transpose(1, 0, 2), species[0], dest_key[0], listed.reshape(1, -1), send_count[0],
        border_rows[None], neighbours[0].transpose(2, 0, 1), semaphores=((8,), (8,)), remote=0,
    )
    hidden = radial_in.shape[2]
    rounded, border_feats, idx, offs, f_e, w_e, pre1, pre2, pooled = call(
        layer_one_kernel,
        [
            ((feats, atoms), bf16), ((feats, count), bf16), ((1, edge_total), jnp.int32),
            ((8, edge_total), f32), ((channels, edge_total), f32), ((3 * channels, edge_total), f32),
            ((hidden, edge_total), f32), ((hidden, edge_total), f32), ((feats, atoms), f32),
        ],
        [((8, edges), f32), ((-(-embedding.shape[0] // 16) * 16, channels), f32)],
        nodes, idx, embedding, radial_in, radial_mid, radial_out_one, mix, mix_out_one,
        product_one, border_rows[None],
    )
    h_two, pre1_two, pre2_two, y_two, ghosts, idx_col = call(
        functools.partial(features_kernel, grid),
        [
            ((3 * hidden, edge_total), bf16), ((hidden, edge_total), f32),
            ((hidden, edge_total), f32), ((8, edge_total), f32), ((8, feats, count), bf16),
            ((edge_total, 1), jnp.int32),
        ],
        [],
        border_feats, offs, idx, radial_in, radial_mid, any_outs=(4,),
        semaphores=((8, 2), (8, 2)), remote=1,
    )
    energy, dlocal, dghosts, dy_two, dw_two = call(
        layer_two_kernel,
        [
            ((1, atoms), f32), ((feats, atoms), f32), ((8, feats, count), bf16),
            ((64, edge_total), f32), ((atoms // L, 7 * channels, edges), bf16),
        ],
        [
            ((feats, total), bf16), ((feats, total), f32), ((channels, atoms), f32),
            ((feats, edge_total), bf16), ((7 * channels, edges), f32),
            ((atoms // L, 7 * channels, edges), bf16), ((feats, L), f32), ((feats, L), f32),
        ],
        rounded, ghosts, idx, idx_col, h_two, y_two, nodes, radial_out_two, mix, mix_out_two,
        product_two, read_lin[None], read_hidden.T, read_out[None], any_outs=(4,),
        semaphores=((atoms // L,),),
    )
    doffs, back = call(
        functools.partial(features_back_kernel, grid),
        [((8, edge_total), f32), ((4, feats, count), bf16)],
        [((7 * channels, edges), bf16), ((4, feats, count), bf16), ((2, feats, count), bf16)],
        dghosts, dw_two, dy_two, pre1_two, pre2_two, offs, radial_in, radial_mid,
        radial_out_two, any_ins=(1,), semaphores=((8, 2), (8, 2), ()), remote=2,
    )
    (dpos,) = call(
        layer_one_back_kernel,
        [((8, total), f32)],
        [
            ((3 * channels, edges), bf16), ((8, edges), f32), ((64, edges), f32),
            ((feats, atoms), f32), ((feats, L), f32), ((16, edges), bf16),
        ],
        dlocal, back, border_col, idx_col, offs, doffs, f_e, w_e, pre1, pre2, pooled,
        radial_in, radial_mid, radial_out_one, mix, mix_out_one, product_one,
    )
    (forces,) = call(
        functools.partial(forces_kernel, grid),
        [((3, atoms), f32)], [((8, 8, L), f32)], dpos, border_col,
        semaphores=((8,), (8,)), remote=3,
    )
    return (energy[None], forces[None, None])


def solution(mesh):
    whole = P()
    in_specs = (
        P("gx", "gy", None, None),
        P("gx", "gy", None),
        P("gx", "gy", None),
        P("gx", "gy", None, None),
        P("gx", "gy", None),
        P("gx", "gy", None),
        P("gx", "gy", None, None),
    ) + (whole,) * 13
    out_specs = (P("gx", "gy", None), P("gx", "gy", None, None))
    return jax.shard_map(
        on_device, mesh=mesh, in_specs=in_specs, out_specs=out_specs, check_vma=False
    )
```
